512 devices in a mesh: dp: 8 (over x, core), seq: 64 (over z, y).
Axes of the slice: x: 4, y: 4, z: 16, core: 2. Of those that a mesh axis runs over, the one named last changes fastest.
Arguments:
- hidden_states: bfloat16 [131072, 4096], P(('dp', 'seq'))
- router_weight: bfloat16 [4096, 128], P('seq'), as said below
- expert_ids: int32 [131072, 8], P(('dp', 'seq')), may hold values from 0 to 127, all different within a row
Outputs:
- balance_loss: float32 [], replicated
- expert_load: float32 [128], replicated
- logit_grad: float32 [131072, 128], P(('dp', 'seq'))
- hidden_grad: bfloat16 [131072, 4096], P(('dp', 'seq'))
- weight_grad: float32 [4096, 128], P('seq')
The draws below stay inside these ranges and needn't reach their ends.
Inputs may be any that keep to these rules, and one draw needn't show every extreme that they name: router_weight has entries of standard deviation about 4096 ** -0.5.
All inputs are finite; a program needn't handle non-finite values.
Results may differ from the reference program's by a relative error of at most 0.0049.
Values may be sent and summed in bfloat16 or wider, within the bound.
No kernel may reach another device: no remote copies, remote signals or barrier semaphores. Data moves between devices by JAX's collectives and lax.ppermute only.
A program may use at most 64 MiB of HBM per device.

```python
import jax
import jax.numpy as jnp
from jax import lax

D = 4096
E = 128
K = 8
TOK_DEV = 256
TOKENS = 131072
N_SEQ = 64


def base_weight(key):
    return jax.random.normal(key, (D, E), jnp.float32)


def draw_router_weight(key, part):
    shaped = base_weight(key)
    return (shaped * D ** (-0.5)).astype(jnp.bfloat16)


def shaped_rows(values, columns, top_boost):
    rows = jnp.arange(TOKENS)
    block = rows // TOK_DEV
    blocks = TOKENS // TOK_DEV
    rise = block.astype(jnp.float32) / max(blocks - 1, 1)
    boost = 1.0 + (top_boost - 1.0) * rise
    favored = block % E
    values = values + boost[:, None] * columns[:, favored].T
    feature_block = jnp.arange(D) // (D // N_SEQ)
    heavy = (block % N_SEQ)[:, None] == feature_block[None, :]
    return jnp.where(heavy, 8.0 * values, values)


def draw_hidden_states(key, part):
    columns = base_weight(key) * D ** (-0.5)
    key = jax.random.fold_in(key, 11)
    values = jnp.clip(jax.random.normal(key, (TOKENS, D), jnp.float32), -6.0, 6.0)
    values = shaped_rows(values, columns, 3.0)
    return values.astype(jnp.bfloat16)


def different_ones(rng, rows, number_of, top, lift):
    ranking = jax.random.permutation(jax.random.fold_in(rng, 1), number_of)
    pull = ranking
    for power in range(3):
        pull = pull * pull // number_of
    pull = pull * lift // number_of
    chance = jax.random.randint(jax.random.fold_in(rng, 2), (rows, number_of), 0, 4096) + pull
    holders = jax.random.permutation(jax.random.fold_in(rng, 3), rows)[jnp.arange(number_of) % rows]
    chance = jnp.where(jnp.arange(rows)[:, None] == holders[None, :], 1 << 14, chance)
    merit = chance * number_of + jnp.arange(number_of)
    return lax.top_k(merit.astype(jnp.int32), top)[1].astype(jnp.int32)


def setup_inputs(seed: int = 0) -> dict:
    streams_of = jax.random.split(jax.random.key(seed), 4)
    hidden_states = draw_hidden_states(jax.random.fold_in(streams_of[3], 71), 0)
    router_weight = draw_router_weight(jax.random.fold_in(streams_of[3], 71), 0)
    expert_ids = different_ones(streams_of[2], TOKENS, E, K, 1024)
    return dict(hidden_states=hidden_states, router_weight=router_weight, expert_ids=expert_ids)


def reference(hidden_states, router_weight, expert_ids):
    logits = jnp.dot(hidden_states, router_weight, preferred_element_type=jnp.float32)
    probs = jax.nn.softmax(logits, axis=-1)
    counts = jnp.zeros((E,), jnp.float32).at[expert_ids.reshape(-1)].add(1.0)
    frac = E * counts / (K * TOKENS)
    prob_mean = jnp.sum(probs, axis=0) / TOKENS
    balance_loss = jnp.sum(frac * prob_mean)
    expert_load = E * prob_mean
    level = jnp.sum(probs * frac[None, :], axis=1, keepdims=True)
    logit_grad = E * probs * (frac[None, :] - level)
    grad_low = logit_grad.astype(jnp.bfloat16)
    hidden_grad = jnp.dot(grad_low, router_weight.T, preferred_element_type=jnp.float32).astype(jnp.bfloat16)
    weight_grad = jnp.dot(hidden_states.T, grad_low, preferred_element_type=jnp.float32)
    return balance_loss, expert_load, logit_grad, hidden_grad, weight_grad
```

```python
import jax
import jax.numpy as jnp
from jax import lax
from jax.sharding import Mesh, PartitionSpec as P

K = 8
F32 = jnp.float32
BF16 = jnp.bfloat16
PIECE = 8


def three_rows(v):
    hi = lax.reduce_precision(v, 8, 7)
    rest = v - hi
    mid = lax.reduce_precision(rest, 8, 7)
    return jnp.stack([hi, mid, rest - mid])


def padded_rows(v, rows):
    return jnp.pad(three_rows(v), ((0, rows - 3), (0, 0))).astype(BF16)


def to_each(a, axes, n):
    spread = jnp.broadcast_to(a[None], (n,) + a.shape)
    return lax.all_to_all(spread, axes, 0, 0, tiled=True)


def shards(hidden_states, router_weight, expert_ids):
    nx, nc, nz, ny = (lax.axis_size(a) for a in ("x", "core", "z", "y"))
    experts = router_weight.shape[1]
    total_tokens = hidden_states.shape[0] * nx * nc * nz * ny
    core = lax.axis_index("core")
    place = lax.axis_index("x") * nc + core
    swap = [(i, nc - 1 - i) for i in range(nc)]

    local_counts = jnp.sum(
        (expert_ids[:, :, None] == jnp.arange(experts, dtype=jnp.int32)[None, None, :]).astype(F32),
        axis=(0, 1),
    )

    mine = lax.dynamic_slice_in_dim(router_weight, place * PIECE, PIECE, 0)
    block = jnp.concatenate([mine, padded_rows(local_counts, 8)], 0)
    got = to_each(block, ("z",), nz)
    counts_z = jnp.sum(got[:, 8:11].astype(F32), axis=(0, 1))
    rows_z = got[:, :8].reshape(nz * PIECE, experts)
    block = jnp.concatenate([rows_z, padded_rows(counts_z, 16)], 0)
    got = to_each(block, ("x", "y"), nx * ny)
    other = lax.ppermute(got, "core", swap)
    n_rows = nz * PIECE
    counts = jnp.sum(got[:, n_rows : n_rows + 3].astype(F32), axis=(0, 1)) + jnp.sum(
        other[:, n_rows : n_rows + 3].astype(F32), axis=(0, 1)
    )
    first = jnp.where(core == 0, got[:, :n_rows], other[:, :n_rows])
    second = jnp.where(core == 0, other[:, :n_rows], got[:, :n_rows])
    both = jnp.stack([first, second]).reshape(nc, nx, ny, nz, PIECE, experts)
    weight = both.transpose(3, 2, 1, 0, 4, 5).reshape(-1, experts)

    logits = jnp.dot(hidden_states, weight, preferred_element_type=F32)
    probs = jax.nn.softmax(logits, axis=-1)
    local_probs = jnp.sum(probs, axis=0)
    frac = experts * counts / (K * total_tokens)
    level = jnp.sum(probs * frac[None, :], axis=1, keepdims=True)
    logit_grad = experts * probs * (frac[None, :] - level)
    grad_low = logit_grad.astype(BF16)
    partial_grad = lax.dot_general(
        hidden_states, grad_low, (((0,), (0,)), ((), ())), preferred_element_type=F32
    )

    parts = partial_grad.reshape(nz, ny, nx, nc, PIECE, experts)
    to_send = jnp.where(core == 0, parts[:, :, :, 1], parts[:, :, :, 0])
    to_keep = jnp.where(core == 0, parts[:, :, :, 0], parts[:, :, :, 1])
    order = (2, 1, 0, 3, 4)
    to_send = to_send.transpose(order).reshape(nx * ny * n_rows, experts).astype(BF16)
    to_keep = to_keep.transpose(order).reshape(nx * ny, n_rows, experts)
    sent = jnp.concatenate([to_send, padded_rows(local_probs, 16)], 0)
    came = lax.ppermute(sent, "core", swap)
    hidden_grad = lax.dot_general(
        grad_low, weight, (((1,), (1,)), ((), ())), preferred_element_type=F32
    ).astype(BF16)
    body = nx * ny * n_rows
    probs_c = local_probs + jnp.sum(came[body : body + 3].astype(F32), axis=0)
    summed = (to_keep + came[:body].reshape(nx * ny, n_rows, experts).astype(F32)).astype(BF16)
    extra = jnp.broadcast_to(padded_rows(probs_c, 16)[None], (nx * ny, 16, experts))
    came = lax.all_to_all(jnp.concatenate([summed, extra], 1), ("x", "y"), 0, 0, tiled=True)
    probs_p = jnp.sum(came[:, n_rows : n_rows + 3].astype(F32), axis=(0, 1))
    summed = jnp.sum(came[:, :n_rows].astype(F32), axis=0).reshape(nz, PIECE, experts).astype(BF16)
    extra = jnp.broadcast_to(padded_rows(probs_p, 8)[None], (nz, 8, experts))
    came = lax.all_to_all(jnp.concatenate([summed, extra], 1), ("z",), 0, 0, tiled=True)
    prob_total = jnp.sum(came[:, 8:11].astype(F32), axis=(0, 1))
    own_rows = jnp.sum(came[:, :8].astype(F32), axis=0)
    weight_grad = to_each(own_rows, ("x", "core"), nx * nc).reshape(-1, experts)

    prob_mean = prob_total / total_tokens
    balance_loss = jnp.sum(frac * prob_mean)
    expert_load = experts * prob_mean
    return (balance_loss, expert_load, logit_grad, hidden_grad, weight_grad)


def solution(mesh):
    fine = Mesh(mesh.devices.reshape(4, 2, 16, 4), ("x", "core", "z", "y"))
    tokens = P(("x", "core", "z", "y"), None)
    rows = P(("z", "y"), None)
    return jax.shard_map(
        shards,
        mesh=fine,
        in_specs=(tokens, rows, tokens),
        out_specs=(P(), P(), tokens, tokens, rows),
        check_vma=False,
    )
```

```python
import functools

import jax
import jax.numpy as jnp
from jax import lax
from jax.experimental import pallas as pl
from jax.experimental.pallas import tpu as pltpu
from jax.sharding import Mesh, PartitionSpec as P

K = 8
F32 = jnp.float32
BF16 = jnp.bfloat16
PIECE = 8
MIB = 1 << 20


def three_rows(v, rows):
    hi = v.astype(BF16).astype(F32)
    mid = (v - hi).astype(BF16).astype(F32)
    low = v - hi - mid
    shape = (rows, v.shape[-1])
    row = lax.broadcasted_iota(jnp.int32, shape, 0)
    return jnp.where(row == 0, hi, jnp.where(row == 1, mid, jnp.where(row == 2, low, 0.0)))


def rows_total(a):
    return jnp.sum(jnp.sum(a.astype(F32), axis=0), axis=0, keepdims=True)


def padded_rows(v, rows):
    hi = lax.reduce_precision(v, 8, 7)
    mid = lax.reduce_precision(v - hi, 8, 7)
    return jnp.pad(jnp.stack([hi, mid, v - hi - mid]), ((0, rows - 3), (0, 0))).astype(BF16)


def call(kernel, outs, ins, scratch=(), flops=0, nbytes=0, limit=8 * MIB):
    return pl.pallas_call(
        kernel,
        out_shape=outs,
        in_specs=ins,
        out_specs=jax.tree.map(lambda _: pl.BlockSpec(memory_space=pltpu.VMEM), outs),
        scratch_shapes=list(scratch),
        compiler_params=pltpu.CompilerParams(vmem_limit_bytes=limit),
        cost_estimate=pl.CostEstimate(flops=flops, bytes_accessed=nbytes, transcendentals=0),
    )


VM = pl.BlockSpec(memory_space=pltpu.VMEM)
SM = pl.BlockSpec(memory_space=pltpu.SMEM)
ANY = pl.BlockSpec(memory_space=pl.ANY)


def first_block(place_ref, ids_ref, weight_ref, out_ref):
    experts = weight_ref.shape[1]
    ids = ids_ref[...]
    expert = lax.broadcasted_iota(jnp.int32, (experts, ids.shape[1]), 0)
    hits = jnp.zeros(expert.shape, F32)
    for k in range(ids.shape[0]):
        hits += jnp.where(ids[k : k + 1] == expert, 1.0, 0.0)
    counts = lax.dot_general(
        jnp.ones((8, ids.shape[1]), BF16),
        hits.astype(BF16),
        (((1,), (1,)), ((), ())),
        preferred_element_type=F32,
    )[:1]
    rows = weight_ref[...].astype(F32)
    mine = jnp.zeros((PIECE, experts), F32)
    for p in range(rows.shape[0] // PIECE):
        mine += jnp.where(place_ref[0] == p, rows[p * PIECE : (p + 1) * PIECE], 0.0)
    block = jnp.concatenate([mine, three_rows(counts, 8)], 0).astype(BF16)
    for z in range(out_ref.shape[0]):
        out_ref[z] = block


def local_part(sizes, total, core_ref, got_ref, other_ref, h_hbm, grad_ref, low_ref, w_ref, send_ref,
               keep_ref, probs_ref, frac_ref, h_ref, sem):
    nx, nc, nz, ny = sizes
    n_rows = nz * PIECE
    fetch = pltpu.make_async_copy(h_hbm, h_ref, sem)
    fetch.start()
    experts = got_ref.shape[2]
    low_core = core_ref[0] == 0
    counts = rows_total(got_ref[:, n_rows:]) + rows_total(other_ref[:, n_rows:])
    frac = experts * counts / (K * total)
    frac_ref[...] = frac
    for x in range(nx):
        for y in range(ny):
            for z in range(0, nz, 2):
                at = pl.ds(z * PIECE, 2 * PIECE)
                a = got_ref[x * ny + y, at].astype(F32)
                b = other_ref[x * ny + y, at].astype(F32)
                one = jnp.where(low_core, a, b)
                two = jnp.where(low_core, b, a)
                for i in range(2):
                    row = (((z + i) * ny + y) * nx + x) * 2 * PIECE
                    half = slice(i * PIECE, (i + 1) * PIECE)
                    w_ref[pl.ds(row, 2 * PIECE)] = jnp.concatenate([one[half], two[half]], 0).astype(BF16)
    fetch.wait()
    logits = jnp.dot(h_ref[...], w_ref[...], preferred_element_type=F32)
    shifted = jnp.exp(logits - jnp.max(logits, axis=1, keepdims=True))
    probs = shifted / jnp.sum(shifted, axis=1, keepdims=True)
    probs_ref[...] = jnp.sum(probs, axis=0, keepdims=True)
    level = jnp.sum(probs * frac, axis=1, keepdims=True)
    grad = experts * probs * (frac - level)
    grad_ref[...] = grad
    low = grad.astype(BF16)
    low_ref[...] = low
    width = 2 * ny * nx * nc * PIECE
    for z in range(0, nz, 2):
        part = lax.dot_general(
            h_ref[:, pl.ds((z // 2) * width, width)], low, (((0,), (0,)), ((), ())), preferred_element_type=F32
        )
        part = part.reshape(2, ny, nx, nc, PIECE, experts)
        for x in range(nx):
            for y in range(ny):
                keep = [jnp.where(low_core, part[i, y, x, 0], part[i, y, x, 1]) for i in range(2)]
                send = [jnp.where(low_core, part[i, y, x, 1], part[i, y, x, 0]) for i in range(2)]
                at = pl.ds((x * ny + y) * n_rows + z * PIECE, 2 * PIECE)
                keep_ref[at] = jnp.concatenate(keep, 0)
                send_ref[at] = jnp.concatenate(send, 0).astype(BF16)
    send_ref[pl.ds(nx * ny * n_rows, 16)] = three_rows(probs_ref[...], 16).astype(BF16)


def after_core(keep_ref, came_ref, probs_ref, out_ref):
    peers, rows = out_ref.shape[0], out_ref.shape[1] - 16
    probs = probs_ref[...] + jnp.sum(came_ref[pl.ds(peers * rows, 16)].astype(F32), axis=0, keepdims=True)
    extra = three_rows(probs, 16).astype(BF16)
    for p in range(peers):
        at = pl.ds(p * rows, rows)
        out_ref[p, :rows] = (keep_ref[at] + came_ref[at].astype(F32)).astype(BF16)
        out_ref[p, rows:] = extra


def after_plane(came_ref, out_ref):
    rows = came_ref.shape[1] - 16
    extra = three_rows(rows_total(came_ref[:, rows:]), 8)
    summed = came_ref[0, :rows].astype(F32)
    for p in range(1, came_ref.shape[0]):
        summed += came_ref[p, :rows].astype(F32)
    for z in range(out_ref.shape[0]):
        out_ref[z] = jnp.concatenate([summed[z * PIECE : (z + 1) * PIECE], extra], 0).astype(BF16)


def after_z(came_ref, out_ref, probs_ref):
    summed = jnp.sum(came_ref[...].astype(F32), axis=0)
    probs_ref[...] = jnp.sum(summed[PIECE:], axis=0, keepdims=True)
    for p in range(out_ref.shape[0]):
        out_ref[p] = summed[:PIECE]


def shards(hidden_states, router_weight, expert_ids):
    sizes = nx, nc, nz, ny = tuple(lax.axis_size(a) for a in ("x", "core", "z", "y"))
    tokens, width = hidden_states.shape
    experts = router_weight.shape[1]
    total_tokens = tokens * nx * nc * nz * ny
    core = lax.axis_index("core").astype(jnp.int32)
    place = lax.axis_index("x").astype(jnp.int32) * nc + core
    swap = [(i, nc - 1 - i) for i in range(nc)]
    plane, n_rows = nx * ny, nz * PIECE

    block = call(first_block, pltpu.VMEM((nz, 16, experts), BF16), [SM, VM, VM])(place[None], expert_ids.T, router_weight)
    got = lax.all_to_all(block, ("z",), 0, 0, tiled=True)
    counts_z = jnp.sum(got[:, 8:].astype(F32), axis=(0, 1))
    block = jnp.concatenate([got[:, :8].reshape(n_rows, experts), padded_rows(counts_z, 16)], 0)
    block = jnp.broadcast_to(block[None], (plane,) + block.shape)
    got = lax.all_to_all(block, ("x", "y"), 0, 0, tiled=True)
    other = lax.ppermute(got, "core", swap)

    grad_out, low, weight, sent, kept, local_probs, frac = call(
        functools.partial(local_part, sizes, total_tokens),
        (
            pltpu.VMEM((tokens, experts), F32),
            pltpu.VMEM((tokens, experts), BF16),
            pltpu.VMEM((width, experts), BF16),
            pltpu.VMEM((plane * n_rows + 16, experts), BF16),
            pltpu.VMEM((plane * n_rows, experts), F32),
            pltpu.VMEM((1, experts), F32),
            pltpu.VMEM((1, experts), F32),
        ),
        [SM, VM, VM, ANY],
        scratch=[pltpu.VMEM((tokens, width), BF16), pltpu.SemaphoreType.DMA],
        flops=4 * tokens * width * experts,
        nbytes=6 * MIB,
        limit=24 * MIB,
    )(core[None], got, other, hidden_states)

    came = lax.ppermute(sent, "core", swap)
    out = pltpu.VMEM((plane, n_rows + 16, experts), BF16)
    block = call(after_core, out, [VM, VM, VM], nbytes=3 * MIB)(kept, came, local_probs)
    came = lax.all_to_all(block, ("x", "y"), 0, 0, tiled=True)
    block = call(after_plane, pltpu.VMEM((nz, 16, experts), BF16), [VM], nbytes=MIB)(came)
    came = lax.all_to_all(block, ("z",), 0, 0, tiled=True)
    out = (pltpu.VMEM((nx * nc, PIECE, experts), F32), pltpu.VMEM((1, experts), F32))
    block, prob_total = call(after_z, out, [VM], nbytes=MIB // 8)(came)
    weight_grad = lax.all_to_all(block, ("x", "core"), 0, 0, tiled=True).reshape(-1, experts)

    hidden_grad = lax.dot_general(
        low, weight, (((1,), (1,)), ((), ())), preferred_element_type=F32
    ).astype(BF16)
    prob_mean = prob_total[0] / total_tokens
    balance_loss = jnp.sum(frac[0] * prob_mean)
    expert_load = experts * prob_mean
    return (balance_loss, expert_load, grad_out, hidden_grad, weight_grad)


def solution(mesh):
    fine = Mesh(mesh.devices.reshape(4, 2, 16, 4), ("x", "core", "z", "y"))
    tokens = P(("x", "core", "z", "y"), None)
    rows = P(("z", "y"), None)
    return jax.shard_map(
        shards,
        mesh=fine,
        in_specs=(tokens, rows, tokens),
        out_specs=(P(), P(), tokens, tokens, rows),
        check_vma=False,
    )
```

```python
import functools

import jax
import jax.numpy as jnp
from jax import lax
from jax.experimental import pallas as pl
from jax.experimental.pallas import tpu as pltpu
from jax.sharding import Mesh, PartitionSpec as P

K = 8
F32 = jnp.float32
BF16 = jnp.bfloat16
PIECE = 8
MIB = 1 << 20


def three_rows(v, rows):
    hi = v.astype(BF16).astype(F32)
    mid = (v - hi).astype(BF16).astype(F32)
    low = v - hi - mid
    shape = (rows, v.shape[-1])
    row = lax.broadcasted_iota(jnp.int32, shape, 0)
    return jnp.where(row == 0, hi, jnp.where(row == 1, mid, jnp.where(row == 2, low, 0.0)))


def rows_total(a):
    return jnp.sum(jnp.sum(a.astype(F32), axis=0), axis=0, keepdims=True)


def padded_rows(v, rows):
    hi = lax.reduce_precision(v, 8, 7)
    mid = lax.reduce_precision(v - hi, 8, 7)
    return jnp.pad(jnp.stack([hi, mid, v - hi - mid]), ((0, rows - 3), (0, 0))).astype(BF16)


def call(kernel, outs, ins, outs_at=None, scratch=(), flops=0, nbytes=0, limit=8 * MIB):
    return pl.pallas_call(
        kernel,
        out_shape=outs,
        in_specs=ins,
        out_specs=outs_at or jax.tree.map(lambda _: VM, outs),
        scratch_shapes=list(scratch),
        compiler_params=pltpu.CompilerParams(vmem_limit_bytes=limit),
        cost_estimate=pl.CostEstimate(flops=flops, bytes_accessed=nbytes, transcendentals=0),
    )


VM = pl.BlockSpec(memory_space=pltpu.VMEM)
SM = pl.BlockSpec(memory_space=pltpu.SMEM)
HBM = pl.BlockSpec(memory_space=pltpu.HBM)


def in_hbm(a):
    return pltpu.with_memory_space_constraint(a, pltpu.HBM)


def first_block(place_ref, ids_hbm, weight_hbm, out_ref, ids_ref, rows_ref, sems):
    pair = pl.multiple_of(place_ref[0] // 2 * (2 * PIECE), 2 * PIECE)
    fetches = [
        pltpu.make_async_copy(ids_hbm, ids_ref, sems.at[0]),
        pltpu.make_async_copy(weight_hbm.at[pl.ds(pair, 2 * PIECE)], rows_ref, sems.at[1]),
    ]
    for fetch in fetches:
        fetch.start()
    for fetch in fetches:
        fetch.wait()
    experts = rows_ref.shape[1]
    expert = lax.broadcasted_iota(jnp.int32, (experts, ids_ref.shape[1]), 0)
    hits = jnp.zeros(expert.shape, F32)
    for k in range(ids_ref.shape[0]):
        hits += jnp.where(ids_ref[k : k + 1] == expert, 1.0, 0.0)
    counts = lax.dot_general(
        jnp.ones((8, ids_ref.shape[1]), BF16),
        hits.astype(BF16),
        (((1,), (1,)), ((), ())),
        preferred_element_type=F32,
    )[:1]
    rows = rows_ref[...].astype(F32)
    mine = jnp.where(place_ref[0] % 2 == 0, rows[:PIECE], rows[PIECE:])
    block = jnp.concatenate([mine, three_rows(counts, 8)], 0).astype(BF16)
    for z in range(out_ref.shape[0]):
        out_ref[z] = block


def local_part(sizes, total, core_ref, got_ref, other_ref, h_ref, grad_hbm, low_ref, w_ref, send_ref,
               keep_ref, probs_ref, frac_ref, grad_ref, sem):
    nx, nc, nz, ny = sizes
    n_rows = nz * PIECE
    experts = got_ref.shape[2]
    low_core = core_ref[0] == 0
    counts = rows_total(got_ref[:, n_rows:]) + rows_total(other_ref[:, n_rows:])
    frac = experts * counts / (K * total)
    frac_ref[...] = frac
    for x in range(nx):
        for y in range(ny):
            for z in range(0, nz, 2):
                at = pl.ds(z * PIECE, 2 * PIECE)
                a = got_ref[x * ny + y, at].astype(F32)
                b = other_ref[x * ny + y, at].astype(F32)
                one = jnp.where(low_core, a, b)
                two = jnp.where(low_core, b, a)
                for i in range(2):
                    row = (((z + i) * ny + y) * nx + x) * 2 * PIECE
                    half = slice(i * PIECE, (i + 1) * PIECE)
                    w_ref[pl.ds(row, 2 * PIECE)] = jnp.concatenate([one[half], two[half]], 0).astype(BF16)
    logits = jnp.dot(h_ref[...], w_ref[...], preferred_element_type=F32)
    shifted = jnp.exp(logits - jnp.max(logits, axis=1, keepdims=True))
    probs = shifted / jnp.sum(shifted, axis=1, keepdims=True)
    probs_ref[...] = jnp.sum(probs, axis=0, keepdims=True)
    level = jnp.sum(probs * frac, axis=1, keepdims=True)
    grad = experts * probs * (frac - level)
    grad_ref[...] = grad
    write = pltpu.make_async_copy(grad_ref, grad_hbm, sem)
    write.start()
    low = grad.astype(BF16)
    low_ref[...] = low
    width = 2 * ny * nx * nc * PIECE
    for z in range(0, nz, 2):
        part = lax.dot_general(
            h_ref[:, pl.ds((z // 2) * width, width)], low, (((0,), (0,)), ((), ())), preferred_element_type=F32
        )
        part = part.reshape(2, ny, nx, nc, PIECE, experts)
        for x in range(nx):
            for y in range(ny):
                keep = [jnp.where(low_core, part[i, y, x, 0], part[i, y, x, 1]) for i in range(2)]
                send = [jnp.where(low_core, part[i, y, x, 1], part[i, y, x, 0]) for i in range(2)]
                at = pl.ds((x * ny + y) * n_rows + z * PIECE, 2 * PIECE)
                keep_ref[at] = jnp.concatenate(keep, 0)
                send_ref[at] = jnp.concatenate(send, 0).astype(BF16)
    send_ref[pl.ds(nx * ny * n_rows, 16)] = three_rows(probs_ref[...], 16).astype(BF16)
    write.wait()


def activation_part(low_ref, w_ref, out_hbm, out_ref, sems):
    width = out_ref.shape[1] // sems.shape[0]
    writes = []
    for i in range(sems.shape[0]):
        at = pl.ds(i * width, width)
        out_ref[:, at] = lax.dot_general(
            low_ref[...], w_ref[at], (((1,), (1,)), ((), ())), preferred_element_type=F32
        ).astype(BF16)
        writes.append(pltpu.make_async_copy(out_ref.at[:, at], out_hbm.at[:, at], sems.at[i]))
        writes[-1].start()
    for write in writes:
        write.wait()


def after_core(keep_ref, came_ref, probs_ref, out_ref):
    peers, rows = out_ref.shape[0], out_ref.shape[1] - 8
    probs = probs_ref[...] + jnp.sum(came_ref[pl.ds(peers * rows, 16)].astype(F32), axis=0, keepdims=True)
    extra = three_rows(probs, 8).astype(BF16)
    for p in range(peers):
        at = pl.ds(p * rows, rows)
        out_ref[p, :rows] = (keep_ref[at] + came_ref[at].astype(F32)).astype(BF16)
        out_ref[p, rows:] = extra


def after_plane(came_ref, out_ref):
    rows = came_ref.shape[1] - 8
    extra = three_rows(rows_total(came_ref[:, rows:]), 8)
    summed = came_ref[0, :rows].astype(F32)
    for p in range(1, came_ref.shape[0]):
        summed += came_ref[p, :rows].astype(F32)
    for z in range(out_ref.shape[0]):
        out_ref[z] = jnp.concatenate([summed[z * PIECE : (z + 1) * PIECE], extra], 0).astype(BF16)


def after_z(came_ref, out_ref, probs_ref):
    summed = jnp.sum(came_ref[...].astype(F32), axis=0)
    probs_ref[...] = jnp.sum(summed[PIECE:], axis=0, keepdims=True)
    for p in range(out_ref.shape[0]):
        out_ref[p] = summed[:PIECE]


def last_part(total, came_ref, probs_ref, frac_ref, grad_ref, load_ref, loss_ref):
    mean = probs_ref[...] / total
    load_ref[...] = came_ref.shape[2] * mean
    loss_ref[...] = jnp.sum(frac_ref[...] * mean, axis=1, keepdims=True)
    for p in range(came_ref.shape[0]):
        grad_ref[pl.ds(p * PIECE, PIECE)] = came_ref[p]


def shards(hidden_states, router_weight, expert_ids):
    sizes = nx, nc, nz, ny = tuple(lax.axis_size(a) for a in ("x", "core", "z", "y"))
    tokens, width = hidden_states.shape
    experts = router_weight.shape[1]
    total_tokens = tokens * nx * nc * nz * ny
    core = lax.axis_index("core").astype(jnp.int32)
    place = lax.axis_index("x").astype(jnp.int32) * nc + core
    swap = [(i, nc - 1 - i) for i in range(nc)]
    plane, n_rows = nx * ny, nz * PIECE
    vm, sds = pltpu.VMEM, jax.ShapeDtypeStruct

    block = call(
        first_block,
        vm((nz, 16, experts), BF16),
        [SM, HBM, HBM],
        scratch=[vm(expert_ids.T.shape, jnp.int32), vm((2 * PIECE, experts), BF16), pltpu.SemaphoreType.DMA((2,))],
    )(place[None], in_hbm(expert_ids.T), in_hbm(router_weight))
    got = lax.all_to_all(block, ("z",), 0, 0, tiled=True)
    counts_z = jnp.sum(got[:, 8:].astype(F32), axis=(0, 1))
    block = jnp.concatenate([got[:, :8].reshape(n_rows, experts), padded_rows(counts_z, 8)], 0)
    block = jnp.broadcast_to(block[None], (plane,) + block.shape)
    got = lax.all_to_all(block, ("x", "y"), 0, 0, tiled=True)
    other = lax.ppermute(got, "core", swap)

    grad_out, low, weight, sent, kept, local_probs, frac = call(
        functools.partial(local_part, sizes, total_tokens),
        (
            sds((tokens, experts), F32),
            vm((tokens, experts), BF16),
            vm((width, experts), BF16),
            vm((plane * n_rows + 16, experts), BF16),
            vm((plane * n_rows, experts), F32),
            vm((1, experts), F32),
            vm((1, experts), F32),
        ),
        [SM, VM, VM, VM],
        outs_at=(HBM,) + (VM,) * 6,
        scratch=[vm((tokens, experts), F32), pltpu.SemaphoreType.DMA],
        flops=4 * tokens * width * experts,
        nbytes=6 * MIB,
        limit=24 * MIB,
    )(core[None], got, other, hidden_states)

    came = lax.ppermute(sent, "core", swap)
    hidden_grad = call(
        activation_part,
        sds((tokens, width), BF16),
        [VM, VM],
        outs_at=HBM,
        scratch=[vm((tokens, width), BF16), pltpu.SemaphoreType.DMA((8,))],
        flops=2 * tokens * width * experts,
        nbytes=3 * MIB,
    )(low, weight)
    came, hidden_grad = lax.optimization_barrier((came, hidden_grad))
    out = vm((plane, n_rows + 8, experts), BF16)
    block = call(after_core, out, [VM, VM, VM], nbytes=3 * MIB)(kept, came, local_probs)
    came = lax.all_to_all(block, ("x", "y"), 0, 0, tiled=True)
    block = call(after_plane, vm((nz, 16, experts), BF16), [VM], nbytes=MIB)(came)
    came = lax.all_to_all(block, ("z",), 0, 0, tiled=True)
    out = (vm((nx * nc, PIECE, experts), F32), vm((1, experts), F32))
    block, prob_total = call(after_z, out, [VM], nbytes=MIB // 8)(came)
    came = lax.all_to_all(block, ("x", "core"), 0, 0, tiled=True)
    out = (sds((nx * nc * PIECE, experts), F32), sds((1, experts), F32), sds((1, 1), F32))
    weight_grad, expert_load, balance_loss = call(
        functools.partial(last_part, total_tokens), out, [VM, VM, VM]
    )(came, prob_total, frac)
    return (balance_loss[0, 0], expert_load[0], grad_out, hidden_grad, weight_grad)


def solution(mesh):
    fine = Mesh(mesh.devices.reshape(4, 2, 16, 4), ("x", "core", "z", "y"))
    tokens = P(("x", "core", "z", "y"), None)
    rows = P(("z", "y"), None)
    return jax.shard_map(
        shards,
        mesh=fine,
        in_specs=(tokens, rows, tokens),
        out_specs=(P(), P(), tokens, tokens, rows),
        check_vma=False,
    )
```

```python
import functools

import jax
import jax.numpy as jnp
from jax import lax
from jax.experimental import pallas as pl
from jax.experimental.pallas import tpu as pltpu
from jax.sharding import Mesh, PartitionSpec as P

K = 8
F32 = jnp.float32
BF16 = jnp.bfloat16
PIECE = 8
MIB = 1 << 20


def three_rows(v, rows):
    hi = v.astype(BF16).astype(F32)
    mid = (v - hi).astype(BF16).astype(F32)
    low = v - hi - mid
    shape = (rows, v.shape[-1])
    row = lax.broadcasted_iota(jnp.int32, shape, 0)
    return jnp.where(row == 0, hi, jnp.where(row == 1, mid, jnp.where(row == 2, low, 0.0)))


def two_rows(v):
    hi = v.astype(BF16).astype(F32)
    row = lax.broadcasted_iota(jnp.int32, (2, v.shape[-1]), 0)
    return jnp.where(row == 0, hi, v - hi)


def put_pairs(out_ref, z, rows, extra):
    experts = rows.shape[1]
    for j in range(PIECE // 2):
        out_ref[z, :, j * experts : (j + 1) * experts] = rows[2 * j : 2 * j + 2].astype(BF16)
    out_ref[z, :, PIECE // 2 * experts :] = extra.astype(BF16)


def rows_total(a):
    return jnp.sum(jnp.sum(a.astype(F32), axis=0), axis=0, keepdims=True)


def call(kernel, outs, ins, outs_at=None, scratch=(), flops=0, nbytes=0, limit=8 * MIB):
    return pl.pallas_call(
        kernel,
        out_shape=outs,
        in_specs=ins,
        out_specs=outs_at or jax.tree.map(lambda _: VM, outs),
        scratch_shapes=list(scratch),
        compiler_params=pltpu.CompilerParams(vmem_limit_bytes=limit),
        cost_estimate=pl.CostEstimate(flops=flops, bytes_accessed=nbytes, transcendentals=0),
    )


VM = pl.BlockSpec(memory_space=pltpu.VMEM)
SM = pl.BlockSpec(memory_space=pltpu.SMEM)
HBM = pl.BlockSpec(memory_space=pltpu.HBM)


def in_hbm(a):
    return pltpu.with_memory_space_constraint(a, pltpu.HBM)


def first_block(place_ref, ids_hbm, weight_hbm, out_ref, ids_ref, rows_ref, sems):
    pair = pl.multiple_of(place_ref[0] // 2 * (2 * PIECE), 2 * PIECE)
    fetches = [
        pltpu.make_async_copy(ids_hbm, ids_ref, sems.at[0]),
        pltpu.make_async_copy(weight_hbm.at[pl.ds(pair, 2 * PIECE)], rows_ref, sems.at[1]),
    ]
    for fetch in fetches:
        fetch.start()
    for fetch in fetches:
        fetch.wait()
    experts = rows_ref.shape[1]
    expert = lax.broadcasted_iota(jnp.int32, (experts, ids_ref.shape[1]), 0)
    hits = jnp.zeros(expert.shape, F32)
    for k in range(ids_ref.shape[0]):
        hits += jnp.where(ids_ref[k : k + 1] == expert, 1.0, 0.0)
    counts = lax.dot_general(
        jnp.ones((8, ids_ref.shape[1]), BF16),
        hits.astype(BF16),
        (((1,), (1,)), ((), ())),
        preferred_element_type=F32,
    )[:1]
    rows = rows_ref[...].astype(F32)
    mine = jnp.where(place_ref[0] % 2 == 0, rows[:PIECE], rows[PIECE:])
    extra = two_rows(counts)
    for z in range(out_ref.shape[0]):
        put_pairs(out_ref, z, mine, extra)


def next_block(came_ref, out_ref):
    nz, experts = came_ref.shape[0], out_ref.shape[2]
    cut = PIECE // 2 * experts
    rows, counts = [], jnp.zeros((2, experts), F32)
    for z in range(nz):
        came = came_ref[z].astype(F32)
        rows += [came[:, j : j + experts] for j in range(0, cut, experts)]
        counts += came[:, cut:]
    block = jnp.concatenate(rows, 0).astype(BF16)
    extra = three_rows(jnp.sum(counts, axis=0, keepdims=True), 8).astype(BF16)
    for p in range(out_ref.shape[0]):
        out_ref[p, : nz * PIECE] = block
        out_ref[p, nz * PIECE :] = extra


def fetch_activations(got_ref, h_hbm, h_ref, sem):
    fetch = pltpu.make_async_copy(h_hbm, h_ref, sem)
    fetch.start()
    fetch.wait()


def local_part(sizes, total, core_ref, got_ref, other_ref, h_ref, grad_hbm, low_ref, w_ref, send_ref,
               keep_ref, probs_ref, frac_ref, grad_ref, sem):
    nx, nc, nz, ny = sizes
    n_rows = nz * PIECE
    experts = got_ref.shape[2]
    low_core = core_ref[0] == 0
    counts = rows_total(got_ref[:, n_rows:]) + rows_total(other_ref[:, n_rows:])
    frac = experts * counts / (K * total)
    frac_ref[...] = frac
    for x in range(nx):
        for y in range(ny):
            for z in range(0, nz, 2):
                at = pl.ds(z * PIECE, 2 * PIECE)
                a = got_ref[x * ny + y, at].astype(F32)
                b = other_ref[x * ny + y, at].astype(F32)
                one = jnp.where(low_core, a, b)
                two = jnp.where(low_core, b, a)
                for i in range(2):
                    row = (((z + i) * ny + y) * nx + x) * 2 * PIECE
                    half = slice(i * PIECE, (i + 1) * PIECE)
                    w_ref[pl.ds(row, 2 * PIECE)] = jnp.concatenate([one[half], two[half]], 0).astype(BF16)
    logits = jnp.dot(h_ref[...], w_ref[...], preferred_element_type=F32)
    shifted = jnp.exp(logits - jnp.max(logits, axis=1, keepdims=True))
    probs = shifted / jnp.sum(shifted, axis=1, keepdims=True)
    probs_ref[...] = jnp.sum(probs, axis=0, keepdims=True)
    level = jnp.sum(probs * frac, axis=1, keepdims=True)
    grad = experts * probs * (frac - level)
    grad_ref[...] = grad
    write = pltpu.make_async_copy(grad_ref, grad_hbm, sem)
    write.start()
    low = grad.astype(BF16)
    low_ref[...] = low
    width = 2 * ny * nx * nc * PIECE
    for z in range(0, nz, 2):
        part = lax.dot_general(
            h_ref[:, pl.ds((z // 2) * width, width)], low, (((0,), (0,)), ((), ())), preferred_element_type=F32
        )
        part = part.reshape(2, ny, nx, nc, PIECE, experts)
        for x in range(nx):
            for y in range(ny):
                keep = [jnp.where(low_core, part[i, y, x, 0], part[i, y, x, 1]) for i in range(2)]
                send = [jnp.where(low_core, part[i, y, x, 1], part[i, y, x, 0]) for i in range(2)]
                at = pl.ds((x * ny + y) * n_rows + z * PIECE, 2 * PIECE)
                keep_ref[at] = jnp.concatenate(keep, 0)
                send_ref[at] = jnp.concatenate(send, 0).astype(BF16)
    send_ref[pl.ds(nx * ny * n_rows, 16)] = three_rows(probs_ref[...], 16).astype(BF16)
    write.wait()


def activation_part(low_ref, w_ref, out_hbm, out_ref, sems):
    width = out_ref.shape[1] // sems.shape[0]
    writes = []
    for i in range(sems.shape[0]):
        at = pl.ds(i * width, width)
        out_ref[:, at] = lax.dot_general(
            low_ref[...], w_ref[at], (((1,), (1,)), ((), ())), preferred_element_type=F32
        ).astype(BF16)
        writes.append(pltpu.make_async_copy(out_ref.at[:, at], out_hbm.at[:, at], sems.at[i]))
        writes[-1].start()
    for write in writes:
        write.wait()


def after_core(keep_ref, came_ref, probs_ref, out_ref):
    peers, rows = out_ref.shape[0], out_ref.shape[1] - 8
    probs = probs_ref[...] + jnp.sum(came_ref[pl.ds(peers * rows, 16)].astype(F32), axis=0, keepdims=True)
    extra = three_rows(probs, 8).astype(BF16)
    for p in range(peers):
        at = pl.ds(p * rows, rows)
        out_ref[p, :rows] = (keep_ref[at] + came_ref[at].astype(F32)).astype(BF16)
        out_ref[p, rows:] = extra


def after_plane(came_ref, out_ref):
    rows = came_ref.shape[1] - 8
    extra = two_rows(rows_total(came_ref[:, rows:]))
    summed = came_ref[0, :rows].astype(F32)
    for p in range(1, came_ref.shape[0]):
        summed += came_ref[p, :rows].astype(F32)
    for z in range(out_ref.shape[0]):
        put_pairs(out_ref, z, summed[z * PIECE : (z + 1) * PIECE], extra)


def after_z(came_ref, out_ref, probs_ref):
    summed = came_ref[0].astype(F32)
    for z in range(1, came_ref.shape[0]):
        summed += came_ref[z].astype(F32)
    experts = out_ref.shape[2]
    cut = PIECE // 2 * experts
    probs_ref[...] = jnp.sum(summed[:, cut:], axis=0, keepdims=True)
    own = jnp.concatenate([summed[:, j : j + experts] for j in range(0, cut, experts)], 0)
    for p in range(out_ref.shape[0]):
        out_ref[p] = own


def last_part(total, came_ref, probs_ref, frac_ref, grad_ref, load_ref, loss_ref):
    mean = probs_ref[...] / total
    load_ref[...] = came_ref.shape[2] * mean
    loss_ref[...] = jnp.sum(frac_ref[...] * mean, axis=1, keepdims=True)
    for p in range(came_ref.shape[0]):
        grad_ref[pl.ds(p * PIECE, PIECE)] = came_ref[p]


def shards(hidden_states, router_weight, expert_ids):
    sizes = nx, nc, nz, ny = tuple(lax.axis_size(a) for a in ("x", "core", "z", "y"))
    tokens, width = hidden_states.shape
    experts = router_weight.shape[1]
    total_tokens = tokens * nx * nc * nz * ny
    core = lax.axis_index("core").astype(jnp.int32)
    place = lax.axis_index("x").astype(jnp.int32) * nc + core
    swap = [(i, nc - 1 - i) for i in range(nc)]
    plane, n_rows = nx * ny, nz * PIECE
    vm, sds = pltpu.VMEM, jax.ShapeDtypeStruct
    pairs = vm((nz, 2, (PIECE // 2 + 1) * experts), BF16)

    block = call(
        first_block,
        pairs,
        [SM, HBM, HBM],
        scratch=[vm(expert_ids.T.shape, jnp.int32), vm((2 * PIECE, experts), BF16), pltpu.SemaphoreType.DMA((2,))],
        nbytes=MIB // 4,
    )(place[None], in_hbm(expert_ids.T), in_hbm(router_weight))
    got = lax.all_to_all(block, ("z",), 0, 0, tiled=True)
    block = call(next_block, vm((plane, n_rows + 8, experts), BF16), [VM], nbytes=MIB)(got)
    got = lax.all_to_all(block, ("x", "y"), 0, 0, tiled=True)
    other = lax.ppermute(got, "core", swap)
    h_near = call(
        fetch_activations,
        vm((tokens, width), BF16),
        [VM, HBM],
        scratch=[pltpu.SemaphoreType.DMA],
        nbytes=4 * MIB,
    )(got, in_hbm(hidden_states))
    other, h_near = lax.optimization_barrier((other, h_near))

    grad_out, low, weight, sent, kept, local_probs, frac = call(
        functools.partial(local_part, sizes, total_tokens),
        (
            sds((tokens, experts), F32),
            vm((tokens, experts), BF16),
            vm((width, experts), BF16),
            vm((plane * n_rows + 16, experts), BF16),
            vm((plane * n_rows, experts), F32),
            vm((1, experts), F32),
            vm((1, experts), F32),
        ),
        [SM, VM, VM, VM],
        outs_at=(HBM,) + (VM,) * 6,
        scratch=[vm((tokens, experts), F32), pltpu.SemaphoreType.DMA],
        flops=4 * tokens * width * experts,
        nbytes=6 * MIB,
        limit=24 * MIB,
    )(core[None], got, other, h_near)

    came = lax.ppermute(sent, "core", swap)
    hidden_grad = call(
        activation_part,
        sds((tokens, width), BF16),
        [VM, VM],
        outs_at=HBM,
        scratch=[vm((tokens, width), BF16), pltpu.SemaphoreType.DMA((8,))],
        flops=2 * tokens * width * experts,
        nbytes=3 * MIB,
    )(low, weight)
    came, hidden_grad = lax.optimization_barrier((came, hidden_grad))
    out = vm((plane, n_rows + 8, experts), BF16)
    block = call(after_core, out, [VM, VM, VM], nbytes=3 * MIB)(kept, came, local_probs)
    came = lax.all_to_all(block, ("x", "y"), 0, 0, tiled=True)
    block = call(after_plane, pairs, [VM], nbytes=MIB)(came)
    came = lax.all_to_all(block, ("z",), 0, 0, tiled=True)
    out = (vm((nx * nc, PIECE, experts), F32), vm((1, experts), F32))
    block, prob_total = call(after_z, out, [VM], nbytes=MIB // 8)(came)
    came = lax.all_to_all(block, ("x", "core"), 0, 0, tiled=True)
    out = (sds((nx * nc * PIECE, experts), F32), sds((1, experts), F32), sds((1, 1), F32))
    weight_grad, expert_load, balance_loss = call(
        functools.partial(last_part, total_tokens), out, [VM, VM, VM]
    )(came, prob_total, frac)
    return (balance_loss[0, 0], expert_load[0], grad_out, hidden_grad, weight_grad)


def solution(mesh):
    fine = Mesh(mesh.devices.reshape(4, 2, 16, 4), ("x", "core", "z", "y"))
    tokens = P(("x", "core", "z", "y"), None)
    rows = P(("z", "y"), None)
    return jax.shard_map(
        shards,
        mesh=fine,
        in_specs=(tokens, rows, tokens),
        out_specs=(P(), P(), tokens, tokens, rows),
        check_vma=False,
    )
```

```python
import functools

import jax
import jax.numpy as jnp
from jax import lax
from jax.experimental import pallas as pl
from jax.experimental.pallas import tpu as pltpu
from jax.sharding import Mesh, PartitionSpec as P

K = 8
F32 = jnp.float32
BF16 = jnp.bfloat16
PIECE = 8
MIB = 1 << 20


def three_rows(v, rows):
    hi = v.astype(BF16).astype(F32)
    mid = (v - hi).astype(BF16).astype(F32)
    low = v - hi - mid
    shape = (rows, v.shape[-1])
    row = lax.broadcasted_iota(jnp.int32, shape, 0)
    return jnp.where(row == 0, hi, jnp.where(row == 1, mid, jnp.where(row == 2, low, 0.0)))


def two_rows(v):
    hi = v.astype(BF16).astype(F32)
    row = lax.broadcasted_iota(jnp.int32, (2, v.shape[-1]), 0)
    return jnp.where(row == 0, hi, v - hi)


def put_pairs(out_ref, z, rows, extra):
    experts = rows.shape[1]
    for j in range(PIECE // 2):
        out_ref[z, :, j * experts : (j + 1) * experts] = rows[2 * j : 2 * j + 2].astype(BF16)
    out_ref[z, :, PIECE // 2 * experts :] = extra.astype(BF16)


def rows_total(a):
    return jnp.sum(jnp.sum(a.astype(F32), axis=0), axis=0, keepdims=True)


def call(kernel, outs, ins, outs_at=None, scratch=(), flops=0, nbytes=0, limit=8 * MIB):
    return pl.pallas_call(
        kernel,
        out_shape=outs,
        in_specs=ins,
        out_specs=outs_at or jax.tree.map(lambda _: VM, outs),
        scratch_shapes=list(scratch),
        compiler_params=pltpu.CompilerParams(vmem_limit_bytes=limit),
        cost_estimate=pl.CostEstimate(flops=flops, bytes_accessed=nbytes, transcendentals=0),
    )


VM = pl.BlockSpec(memory_space=pltpu.VMEM)
SM = pl.BlockSpec(memory_space=pltpu.SMEM)
HBM = pl.BlockSpec(memory_space=pltpu.HBM)


def in_hbm(a):
    return pltpu.with_memory_space_constraint(a, pltpu.HBM)


def first_block(place_ref, ids_hbm, weight_hbm, out_ref, ids_ref, rows_ref, sems):
    pair = pl.multiple_of(place_ref[0] // 2 * (2 * PIECE), 2 * PIECE)
    fetches = [
        pltpu.make_async_copy(ids_hbm, ids_ref, sems.at[0]),
        pltpu.make_async_copy(weight_hbm.at[pl.ds(pair, 2 * PIECE)], rows_ref, sems.at[1]),
    ]
    for fetch in fetches:
        fetch.start()
    for fetch in fetches:
        fetch.wait()
    experts = rows_ref.shape[1]
    expert = lax.broadcasted_iota(jnp.int32, (experts, ids_ref.shape[1]), 0)
    hits = jnp.zeros(expert.shape, F32)
    for k in range(ids_ref.shape[0]):
        hits += jnp.where(ids_ref[k : k + 1] == expert, 1.0, 0.0)
    counts = lax.dot_general(
        jnp.ones((8, ids_ref.shape[1]), BF16),
        hits.astype(BF16),
        (((1,), (1,)), ((), ())),
        preferred_element_type=F32,
    )[:1]
    rows = rows_ref[...].astype(F32)
    mine = jnp.where(place_ref[0] % 2 == 0, rows[:PIECE], rows[PIECE:])
    extra = two_rows(counts)
    for z in range(out_ref.shape[0]):
        put_pairs(out_ref, z, mine, extra)


def next_block(came_ref, out_ref):
    nz, experts = came_ref.shape[0], out_ref.shape[2]
    cut = PIECE // 2 * experts
    rows, counts = [], jnp.zeros((2, experts), F32)
    for z in range(nz):
        came = came_ref[z].astype(F32)
        rows += [came[:, j : j + experts] for j in range(0, cut, experts)]
        counts += came[:, cut:]
    block = jnp.concatenate(rows, 0).astype(BF16)
    extra = three_rows(jnp.sum(counts, axis=0, keepdims=True), 8).astype(BF16)
    for p in range(out_ref.shape[0]):
        out_ref[p, : nz * PIECE] = block
        out_ref[p, nz * PIECE :] = extra


def fetch_activations(got_ref, h_hbm, h_ref, sem):
    fetch = pltpu.make_async_copy(h_hbm, h_ref, sem)
    fetch.start()
    fetch.wait()


def local_part(sizes, total, core_ref, got_ref, other_ref, h_ref, grad_ref, low_ref, w_ref, send_ref,
               keep_ref, probs_ref, frac_ref):
    nx, nc, nz, ny = sizes
    n_rows = nz * PIECE
    experts = got_ref.shape[2]
    low_core = core_ref[0] == 0
    counts = rows_total(got_ref[:, n_rows:]) + rows_total(other_ref[:, n_rows:])
    frac = experts * counts / (K * total)
    frac_ref[...] = frac
    for x in range(nx):
        for y in range(ny):
            for z in range(0, nz, 2):
                at = pl.ds(z * PIECE, 2 * PIECE)
                a = got_ref[x * ny + y, at].astype(F32)
                b = other_ref[x * ny + y, at].astype(F32)
                one = jnp.where(low_core, a, b)
                two = jnp.where(low_core, b, a)
                for i in range(2):
                    row = (((z + i) * ny + y) * nx + x) * 2 * PIECE
                    half = slice(i * PIECE, (i + 1) * PIECE)
                    w_ref[pl.ds(row, 2 * PIECE)] = jnp.concatenate([one[half], two[half]], 0).astype(BF16)
    logits = jnp.dot(h_ref[...], w_ref[...], preferred_element_type=F32)
    shifted = jnp.exp(logits - jnp.max(logits, axis=1, keepdims=True))
    scale = 1.0 / jnp.sum(shifted, axis=1, keepdims=True)
    level = jnp.sum(shifted * frac, axis=1, keepdims=True) * scale
    probs = shifted * scale
    probs_ref[...] = jnp.sum(probs, axis=0, keepdims=True)
    grad = experts * probs * (frac - level)
    grad_ref[...] = grad
    low = grad.astype(BF16)
    low_ref[...] = low
    width = 2 * ny * nx * nc * PIECE
    for z in range(0, nz, 2):
        part = lax.dot_general(
            h_ref[:, pl.ds((z // 2) * width, width)], low, (((0,), (0,)), ((), ())), preferred_element_type=F32
        )
        part = part.reshape(2, ny, nx, nc, PIECE, experts)
        for x in range(nx):
            for y in range(ny):
                keep = [jnp.where(low_core, part[i, y, x, 0], part[i, y, x, 1]) for i in range(2)]
                send = [jnp.where(low_core, part[i, y, x, 1], part[i, y, x, 0]) for i in range(2)]
                at = pl.ds((x * ny + y) * n_rows + z * PIECE, 2 * PIECE)
                keep_ref[at] = jnp.concatenate(keep, 0)
                send_ref[at] = jnp.concatenate(send, 0).astype(BF16)
    send_ref[pl.ds(nx * ny * n_rows, 16)] = three_rows(probs_ref[...], 16).astype(BF16)


def activation_part(low_ref, w_ref, grad_ref, out_hbm, grad_hbm, out_ref, sems):
    steps = sems.shape[0] - 1
    width = out_ref.shape[1] // steps
    writes = [pltpu.make_async_copy(grad_ref, grad_hbm, sems.at[steps])]
    writes[0].start()
    for i in range(steps):
        at = pl.ds(i * width, width)
        out_ref[:, at] = lax.dot_general(
            low_ref[...], w_ref[at], (((1,), (1,)), ((), ())), preferred_element_type=F32
        ).astype(BF16)
        writes.append(pltpu.make_async_copy(out_ref.at[:, at], out_hbm.at[:, at], sems.at[i]))
        writes[-1].start()
    for write in writes:
        write.wait()


def after_core(keep_ref, came_ref, probs_ref, out_ref):
    peers, rows = out_ref.shape[0], out_ref.shape[1] - 8
    probs = probs_ref[...] + jnp.sum(came_ref[pl.ds(peers * rows, 16)].astype(F32), axis=0, keepdims=True)
    extra = three_rows(probs, 8).astype(BF16)
    for p in range(peers):
        at = pl.ds(p * rows, rows)
        out_ref[p, :rows] = (keep_ref[at] + came_ref[at].astype(F32)).astype(BF16)
        out_ref[p, rows:] = extra


def after_plane(came_ref, out_ref):
    rows = came_ref.shape[1] - 8
    extra = two_rows(rows_total(came_ref[:, rows:]))
    summed = came_ref[0, :rows].astype(F32)
    for p in range(1, came_ref.shape[0]):
        summed += came_ref[p, :rows].astype(F32)
    for z in range(out_ref.shape[0]):
        put_pairs(out_ref, z, summed[z * PIECE : (z + 1) * PIECE], extra)


def after_z(came_ref, out_ref, probs_ref):
    summed = came_ref[0].astype(F32)
    for z in range(1, came_ref.shape[0]):
        summed += came_ref[z].astype(F32)
    experts = out_ref.shape[2]
    cut = PIECE // 2 * experts
    probs_ref[...] = jnp.sum(summed[:, cut:], axis=0, keepdims=True)
    own = jnp.concatenate([summed[:, j : j + experts] for j in range(0, cut, experts)], 0)
    for p in range(out_ref.shape[0]):
        out_ref[p] = own


def last_part(total, came_ref, probs_ref, frac_ref, grad_ref, load_ref, loss_ref):
    mean = probs_ref[...] / total
    load_ref[...] = came_ref.shape[2] * mean
    loss_ref[...] = jnp.sum(frac_ref[...] * mean, axis=1, keepdims=True)
    for p in range(came_ref.shape[0]):
        grad_ref[pl.ds(p * PIECE, PIECE)] = came_ref[p]


def shards(hidden_states, router_weight, expert_ids):
    sizes = nx, nc, nz, ny = tuple(lax.axis_size(a) for a in ("x", "core", "z", "y"))
    tokens, width = hidden_states.shape
    experts = router_weight.shape[1]
    total_tokens = tokens * nx * nc * nz * ny
    core = lax.axis_index("core").astype(jnp.int32)
    place = lax.axis_index("x").astype(jnp.int32) * nc + core
    swap = [(i, nc - 1 - i) for i in range(nc)]
    plane, n_rows = nx * ny, nz * PIECE
    vm, sds = pltpu.VMEM, jax.ShapeDtypeStruct
    pairs = vm((nz, 2, (PIECE // 2 + 1) * experts), BF16)

    block = call(
        first_block,
        pairs,
        [SM, HBM, HBM],
        scratch=[vm(expert_ids.T.shape, jnp.int32), vm((2 * PIECE, experts), BF16), pltpu.SemaphoreType.DMA((2,))],
        nbytes=MIB // 4,
    )(place[None], in_hbm(expert_ids.T), in_hbm(router_weight))
    got = lax.all_to_all(block, ("z",), 0, 0, tiled=True)
    block = call(next_block, vm((plane, n_rows + 8, experts), BF16), [VM], nbytes=MIB)(got)
    got = lax.all_to_all(block, ("x", "y"), 0, 0, tiled=True)
    other = lax.ppermute(got, "core", swap)
    h_near = call(
        fetch_activations,
        vm((tokens, width), BF16),
        [VM, HBM],
        scratch=[pltpu.SemaphoreType.DMA],
        nbytes=4 * MIB,
    )(got, in_hbm(hidden_states))
    other, h_near = lax.optimization_barrier((other, h_near))

    grad_near, low, weight, sent, kept, local_probs, frac = call(
        functools.partial(local_part, sizes, total_tokens),
        (
            vm((tokens, experts), F32),
            vm((tokens, experts), BF16),
            vm((width, experts), BF16),
            vm((plane * n_rows + 16, experts), BF16),
            vm((plane * n_rows, experts), F32),
            vm((1, experts), F32),
            vm((1, experts), F32),
        ),
        [SM, VM, VM, VM],
        flops=4 * tokens * width * experts,
        nbytes=6 * MIB,
        limit=24 * MIB,
    )(core[None], got, other, h_near)

    came = lax.ppermute(sent, "core", swap)
    hidden_grad, grad_out = call(
        activation_part,
        (sds((tokens, width), BF16), sds((tokens, experts), F32)),
        [VM, VM, VM],
        outs_at=(HBM, HBM),
        scratch=[vm((tokens, width), BF16), pltpu.SemaphoreType.DMA((9,))],
        flops=2 * tokens * width * experts,
        nbytes=3 * MIB,
    )(low, weight, grad_near)
    came, hidden_grad, grad_out = lax.optimization_barrier((came, hidden_grad, grad_out))
    out = vm((plane, n_rows + 8, experts), BF16)
    block = call(after_core, out, [VM, VM, VM], nbytes=3 * MIB)(kept, came, local_probs)
    came = lax.all_to_all(block, ("x", "y"), 0, 0, tiled=True)
    block = call(after_plane, pairs, [VM], nbytes=MIB)(came)
    came = lax.all_to_all(block, ("z",), 0, 0, tiled=True)
    out = (vm((nx * nc, PIECE, experts), F32), vm((1, experts), F32))
    block, prob_total = call(after_z, out, [VM], nbytes=MIB // 8)(came)
    came = lax.all_to_all(block, ("x", "core"), 0, 0, tiled=True)
    out = (sds((nx * nc * PIECE, experts), F32), sds((1, experts), F32), sds((1, 1), F32))
    weight_grad, expert_load, balance_loss = call(
        functools.partial(last_part, total_tokens), out, [VM, VM, VM]
    )(came, prob_total, frac)
    return (balance_loss[0, 0], expert_load[0], grad_out, hidden_grad, weight_grad)


def solution(mesh):
    fine = Mesh(mesh.devices.reshape(4, 2, 16, 4), ("x", "core", "z", "y"))
    tokens = P(("x", "core", "z", "y"), None)
    rows = P(("z", "y"), None)
    return jax.shard_map(
        shards,
        mesh=fine,
        in_specs=(tokens, rows, tokens),
        out_specs=(P(), P(), tokens, tokens, rows),
        check_vma=False,
    )
```

```python
import functools

import jax
import jax.numpy as jnp
from jax import lax
from jax.experimental import pallas as pl
from jax.experimental.pallas import tpu as pltpu
from jax.sharding import Mesh, PartitionSpec as P

K = 8
F32 = jnp.float32
BF16 = jnp.bfloat16
PIECE = 8
MIB = 1 << 20


def three_rows(v, rows):
    hi = v.astype(BF16).astype(F32)
    mid = (v - hi).astype(BF16).astype(F32)
    low = v - hi - mid
    shape = (rows, v.shape[-1])
    row = lax.broadcasted_iota(jnp.int32, shape, 0)
    return jnp.where(row == 0, hi, jnp.where(row == 1, mid, jnp.where(row == 2, low, 0.0)))


def two_rows(v):
    hi = v.astype(BF16).astype(F32)
    row = lax.broadcasted_iota(jnp.int32, (2, v.shape[-1]), 0)
    return jnp.where(row == 0, hi, v - hi)


def put_pairs(out_ref, z, rows, extra):
    experts = rows.shape[1]
    for j in range(PIECE // 2):
        out_ref[z, :, j * experts : (j + 1) * experts] = rows[2 * j : 2 * j + 2].astype(BF16)
    out_ref[z, :, PIECE // 2 * experts :] = extra.astype(BF16)


def rows_total(a):
    return jnp.sum(jnp.sum(a.astype(F32), axis=0), axis=0, keepdims=True)


def call(kernel, outs, ins, outs_at=None, scratch=(), flops=0, nbytes=0, limit=8 * MIB):
    return pl.pallas_call(
        kernel,
        out_shape=outs,
        in_specs=ins,
        out_specs=outs_at or jax.tree.map(lambda _: VM, outs),
        scratch_shapes=list(scratch),
        compiler_params=pltpu.CompilerParams(vmem_limit_bytes=limit),
        cost_estimate=pl.CostEstimate(flops=flops, bytes_accessed=nbytes, transcendentals=0),
    )


VM = pl.BlockSpec(memory_space=pltpu.VMEM)
SM = pl.BlockSpec(memory_space=pltpu.SMEM)
HBM = pl.BlockSpec(memory_space=pltpu.HBM)


def in_hbm(a):
    return pltpu.with_memory_space_constraint(a, pltpu.HBM)


def first_block(place_ref, ids_hbm, weight_hbm, out_ref, ids_ref, rows_ref, sems):
    pair = pl.multiple_of(place_ref[0] // 2 * (2 * PIECE), 2 * PIECE)
    fetches = [
        pltpu.make_async_copy(ids_hbm, ids_ref, sems.at[0]),
        pltpu.make_async_copy(weight_hbm.at[pl.ds(pair, 2 * PIECE)], rows_ref, sems.at[1]),
    ]
    for fetch in fetches:
        fetch.start()
    for fetch in fetches:
        fetch.wait()
    experts = rows_ref.shape[1]
    expert = lax.broadcasted_iota(jnp.int32, (experts, ids_ref.shape[1]), 0)
    hits = jnp.zeros(expert.shape, F32)
    for k in range(ids_ref.shape[0]):
        hits += jnp.where(ids_ref[k : k + 1] == expert, 1.0, 0.0)
    counts = lax.dot_general(
        jnp.ones((8, ids_ref.shape[1]), BF16),
        hits.astype(BF16),
        (((1,), (1,)), ((), ())),
        preferred_element_type=F32,
    )[:1]
    rows = rows_ref[...].astype(F32)
    mine = jnp.where(place_ref[0] % 2 == 0, rows[:PIECE], rows[PIECE:])
    extra = two_rows(counts)
    for z in range(out_ref.shape[0]):
        put_pairs(out_ref, z, mine, extra)


def next_block(came_ref, out_ref):
    nz, experts = came_ref.shape[0], out_ref.shape[2]
    cut = PIECE // 2 * experts
    rows, counts = [], jnp.zeros((2, experts), F32)
    for z in range(nz):
        came = came_ref[z].astype(F32)
        rows += [came[:, j : j + experts] for j in range(0, cut, experts)]
        counts += came[:, cut:]
    block = jnp.concatenate(rows, 0).astype(BF16)
    extra = three_rows(jnp.sum(counts, axis=0, keepdims=True), 8).astype(BF16)
    for p in range(out_ref.shape[0]):
        out_ref[p, : nz * PIECE] = block
        out_ref[p, nz * PIECE :] = extra


def fetch_activations(got_ref, h_hbm, h_ref, sem):
    fetch = pltpu.make_async_copy(h_hbm, h_ref, sem)
    fetch.start()
    fetch.wait()


def local_part(sizes, total, core_ref, got_ref, other_ref, h_ref, grad_ref, low_ref, w_ref, send_ref,
               keep_ref, probs_ref, frac_ref):
    nx, nc, nz, ny = sizes
    n_rows = nz * PIECE
    experts = got_ref.shape[2]
    low_core = core_ref[0] == 0
    counts = rows_total(got_ref[:, n_rows:]) + rows_total(other_ref[:, n_rows:])
    frac = experts * counts / (K * total)
    frac_ref[...] = frac
    for x in range(nx):
        for y in range(ny):
            for z in range(0, nz, 2):
                at = pl.ds(z * PIECE, 2 * PIECE)
                a = got_ref[y * nx + x, at].astype(F32)
                b = other_ref[y * nx + x, at].astype(F32)
                one = jnp.where(low_core, a, b)
                two = jnp.where(low_core, b, a)
                for i in range(2):
                    row = (((z + i) * ny + y) * nx + x) * 2 * PIECE
                    half = slice(i * PIECE, (i + 1) * PIECE)
                    w_ref[pl.ds(row, 2 * PIECE)] = jnp.concatenate([one[half], two[half]], 0).astype(BF16)
    logits = jnp.dot(h_ref[...], w_ref[...], preferred_element_type=F32)
    shifted = jnp.exp(logits - jnp.max(logits, axis=1, keepdims=True))
    scale = 1.0 / jnp.sum(shifted, axis=1, keepdims=True)
    level = jnp.sum(shifted * frac, axis=1, keepdims=True) * scale
    probs = shifted * scale
    probs_ref[...] = jnp.sum(probs, axis=0, keepdims=True)
    grad = experts * probs * (frac - level)
    grad_ref[...] = grad
    low = grad.astype(BF16)
    low_ref[...] = low
    width = 2 * ny * nx * nc * PIECE
    for z in range(0, nz, 2):
        part = lax.dot_general(
            h_ref[:, pl.ds((z // 2) * width, width)], low, (((0,), (0,)), ((), ())), preferred_element_type=F32
        )
        part = part.reshape(2, ny, nx, nc, PIECE, experts)
        for x in range(nx):
            for y in range(ny):
                keep = [jnp.where(low_core, part[i, y, x, 0], part[i, y, x, 1]) for i in range(2)]
                send = [jnp.where(low_core, part[i, y, x, 1], part[i, y, x, 0]) for i in range(2)]
                at = pl.ds((y * nx + x) * n_rows + z * PIECE, 2 * PIECE)
                keep_ref[at] = jnp.concatenate(keep, 0)
                send_ref[at] = jnp.concatenate(send, 0).astype(BF16)
    send_ref[pl.ds(nx * ny * n_rows, 16)] = three_rows(probs_ref[...], 16).astype(BF16)


def activation_part(low_ref, w_ref, grad_ref, out_hbm, grad_hbm, out_ref, sems):
    steps = sems.shape[0] - 1
    width = out_ref.shape[1] // steps
    writes = [pltpu.make_async_copy(grad_ref, grad_hbm, sems.at[steps])]
    writes[0].start()
    for i in range(steps):
        at = pl.ds(i * width, width)
        out_ref[:, at] = lax.dot_general(
            low_ref[...], w_ref[at], (((1,), (1,)), ((), ())), preferred_element_type=F32
        ).astype(BF16)
        writes.append(pltpu.make_async_copy(out_ref.at[:, at], out_hbm.at[:, at], sems.at[i]))
        writes[-1].start()
    for write in writes:
        write.wait()


def after_core(keep_ref, came_ref, probs_ref, out_ref):
    peers, rows = out_ref.shape[0], out_ref.shape[1] - 8
    probs = probs_ref[...] + jnp.sum(came_ref[pl.ds(peers * rows, 16)].astype(F32), axis=0, keepdims=True)
    extra = three_rows(probs, 8).astype(BF16)
    for p in range(peers):
        at = pl.ds(p * rows, rows)
        out_ref[p, :rows] = (keep_ref[at] + came_ref[at].astype(F32)).astype(BF16)
        out_ref[p, rows:] = extra


def after_plane(came_ref, out_ref):
    rows = came_ref.shape[1] - 8
    extra = two_rows(rows_total(came_ref[:, rows:]))
    summed = came_ref[0, :rows].astype(F32)
    for p in range(1, came_ref.shape[0]):
        summed += came_ref[p, :rows].astype(F32)
    for z in range(out_ref.shape[0]):
        put_pairs(out_ref, z, summed[z * PIECE : (z + 1) * PIECE], extra)


def after_z(came_ref, out_ref, probs_ref):
    summed = came_ref[0].astype(F32)
    for z in range(1, came_ref.shape[0]):
        summed += came_ref[z].astype(F32)
    experts = out_ref.shape[2]
    cut = PIECE // 2 * experts
    probs_ref[...] = jnp.sum(summed[:, cut:], axis=0, keepdims=True)
    own = jnp.concatenate([summed[:, j : j + experts] for j in range(0, cut, experts)], 0)
    for p in range(out_ref.shape[0]):
        out_ref[p] = own


def last_part(total, came_ref, probs_ref, frac_ref, grad_ref, load_ref, loss_ref):
    mean = probs_ref[...] / total
    load_ref[...] = came_ref.shape[2] * mean
    loss_ref[...] = jnp.sum(frac_ref[...] * mean, axis=1, keepdims=True)
    for p in range(came_ref.shape[0]):
        grad_ref[pl.ds(p * PIECE, PIECE)] = came_ref[p]


def shards(hidden_states, router_weight, expert_ids):
    sizes = nx, nc, nz, ny = tuple(lax.axis_size(a) for a in ("x", "core", "z", "y"))
    tokens, width = hidden_states.shape
    experts = router_weight.shape[1]
    total_tokens = tokens * nx * nc * nz * ny
    core = lax.axis_index("core").astype(jnp.int32)
    place = lax.axis_index("x").astype(jnp.int32) * nc + core
    swap = [(i, nc - 1 - i) for i in range(nc)]
    plane, n_rows = nx * ny, nz * PIECE
    vm, sds = pltpu.VMEM, jax.ShapeDtypeStruct
    pairs = vm((nz, 2, (PIECE // 2 + 1) * experts), BF16)

    block = call(
        first_block,
        pairs,
        [SM, HBM, HBM],
        scratch=[vm(expert_ids.T.shape, jnp.int32), vm((2 * PIECE, experts), BF16), pltpu.SemaphoreType.DMA((2,))],
        nbytes=MIB // 4,
    )(place[None], in_hbm(expert_ids.T), in_hbm(router_weight))
    got = lax.all_to_all(block, ("z",), 0, 0, tiled=True)
    block = call(next_block, vm((plane, n_rows + 8, experts), BF16), [VM], nbytes=MIB)(got)
    got = lax.all_to_all(block, ("y", "x"), 0, 0, tiled=True)
    other = lax.ppermute(got, "core", swap)
    h_near = call(
        fetch_activations,
        vm((tokens, width), BF16),
        [VM, HBM],
        scratch=[pltpu.SemaphoreType.DMA],
        nbytes=4 * MIB,
    )(got, in_hbm(hidden_states))
    other, h_near = lax.optimization_barrier((other, h_near))

    grad_near, low, weight, sent, kept, local_probs, frac = call(
        functools.partial(local_part, sizes, total_tokens),
        (
            vm((tokens, experts), F32),
            vm((tokens, experts), BF16),
            vm((width, experts), BF16),
            vm((plane * n_rows + 16, experts), BF16),
            vm((plane * n_rows, experts), F32),
            vm((1, experts), F32),
            vm((1, experts), F32),
        ),
        [SM, VM, VM, VM],
        flops=4 * tokens * width * experts,
        nbytes=6 * MIB,
        limit=24 * MIB,
    )(core[None], got, other, h_near)

    came = lax.ppermute(sent, "core", swap)
    hidden_grad, grad_out = call(
        activation_part,
        (sds((tokens, width), BF16), sds((tokens, experts), F32)),
        [VM, VM, VM],
        outs_at=(HBM, HBM),
        scratch=[vm((tokens, width), BF16), pltpu.SemaphoreType.DMA((9,))],
        flops=2 * tokens * width * experts,
        nbytes=3 * MIB,
    )(low, weight, grad_near)
    came, hidden_grad, grad_out = lax.optimization_barrier((came, hidden_grad, grad_out))
    out = vm((plane, n_rows + 8, experts), BF16)
    block = call(after_core, out, [VM, VM, VM], nbytes=3 * MIB)(kept, came, local_probs)
    came = lax.all_to_all(block, ("y", "x"), 0, 0, tiled=True)
    block = call(after_plane, pairs, [VM], nbytes=MIB)(came)
    came = lax.all_to_all(block, ("z",), 0, 0, tiled=True)
    out = (vm((nx * nc, PIECE, experts), F32), vm((1, experts), F32))
    block, prob_total = call(after_z, out, [VM], nbytes=MIB // 8)(came)
    came = lax.all_to_all(block, ("x", "core"), 0, 0, tiled=True)
    out = (sds((nx * nc * PIECE, experts), F32), sds((1, experts), F32), sds((1, 1), F32))
    weight_grad, expert_load, balance_loss = call(
        functools.partial(last_part, total_tokens), out, [VM, VM, VM]
    )(came, prob_total, frac)
    return (balance_loss[0, 0], expert_load[0], grad_out, hidden_grad, weight_grad)


def solution(mesh):
    fine = Mesh(mesh.devices.reshape(4, 2, 16, 4), ("x", "core", "z", "y"))
    tokens = P(("x", "core", "z", "y"), None)
    rows = P(("z", "y"), None)
    return jax.shard_map(
        shards,
        mesh=fine,
        in_specs=(tokens, rows, tokens),
        out_specs=(P(), P(), tokens, tokens, rows),
        check_vma=False,
    )
```

```python
import functools

import jax
import jax.numpy as jnp
from jax import lax
from jax.experimental import pallas as pl
from jax.experimental.pallas import tpu as pltpu
from jax.sharding import Mesh, PartitionSpec as P

K = 8
F32 = jnp.float32
BF16 = jnp.bfloat16
PIECE = 8
MIB = 1 << 20


def three_rows(v, rows):
    hi = v.astype(BF16).astype(F32)
    mid = (v - hi).astype(BF16).astype(F32)
    low = v - hi - mid
    shape = (rows, v.shape[-1])
    row = lax.broadcasted_iota(jnp.int32, shape, 0)
    return jnp.where(row == 0, hi, jnp.where(row == 1, mid, jnp.where(row == 2, low, 0.0)))


def two_rows(v):
    hi = v.astype(BF16).astype(F32)
    row = lax.broadcasted_iota(jnp.int32, (2, v.shape[-1]), 0)
    return jnp.where(row == 0, hi, v - hi)


def put_pairs(out_ref, z, rows, extra):
    experts = rows.shape[1]
    for j in range(PIECE // 2):
        out_ref[z, :, j * experts : (j + 1) * experts] = rows[2 * j : 2 * j + 2].astype(BF16)
    out_ref[z, :, PIECE // 2 * experts :] = extra.astype(BF16)


def crossed(n_cores, others):
    chips = [(i, j) for i in range(others[0]) for j in range(others[1])]
    first = [i * 2 // others[0] for i, _ in chips]
    return [[(g ^ h) * len(chips) + n for n, h in enumerate(first)] for g in range(n_cores)]


def rows_total(a):
    return jnp.sum(jnp.sum(a.astype(F32), axis=0), axis=0, keepdims=True)


def call(kernel, outs, ins, outs_at=None, scratch=(), flops=0, nbytes=0, limit=8 * MIB):
    return pl.pallas_call(
        kernel,
        out_shape=outs,
        in_specs=ins,
        out_specs=outs_at or jax.tree.map(lambda _: VM, outs),
        scratch_shapes=list(scratch),
        compiler_params=pltpu.CompilerParams(vmem_limit_bytes=limit),
        cost_estimate=pl.CostEstimate(flops=flops, bytes_accessed=nbytes, transcendentals=0),
    )


VM = pl.BlockSpec(memory_space=pltpu.VMEM)
SM = pl.BlockSpec(memory_space=pltpu.SMEM)
HBM = pl.BlockSpec(memory_space=pltpu.HBM)


def in_hbm(a):
    return pltpu.with_memory_space_constraint(a, pltpu.HBM)


def first_block(place_ref, ids_hbm, weight_hbm, out_ref, ids_ref, rows_ref, sems):
    pair = pl.multiple_of(place_ref[0] // 2 * (2 * PIECE), 2 * PIECE)
    fetches = [
        pltpu.make_async_copy(ids_hbm, ids_ref, sems.at[0]),
        pltpu.make_async_copy(weight_hbm.at[pl.ds(pair, 2 * PIECE)], rows_ref, sems.at[1]),
    ]
    for fetch in fetches:
        fetch.start()
    for fetch in fetches:
        fetch.wait()
    experts = rows_ref.shape[1]
    expert = lax.broadcasted_iota(jnp.int32, (experts, ids_ref.shape[1]), 0)
    hits = jnp.zeros(expert.shape, F32)
    for k in range(ids_ref.shape[0]):
        hits += jnp.where(ids_ref[k : k + 1] == expert, 1.0, 0.0)
    counts = lax.dot_general(
        jnp.ones((8, ids_ref.shape[1]), BF16),
        hits.astype(BF16),
        (((1,), (1,)), ((), ())),
        preferred_element_type=F32,
    )[:1]
    rows = rows_ref[...].astype(F32)
    mine = jnp.where(place_ref[0] % 2 == 0, rows[:PIECE], rows[PIECE:])
    extra = two_rows(counts)
    for z in range(out_ref.shape[0]):
        put_pairs(out_ref, z, mine, extra)


def next_block(came_ref, out_ref):
    nz, experts = came_ref.shape[0], out_ref.shape[2]
    cut = PIECE // 2 * experts
    rows, counts = [], jnp.zeros((2, experts), F32)
    for z in range(nz):
        came = came_ref[z].astype(F32)
        rows += [came[:, j : j + experts] for j in range(0, cut, experts)]
        counts += came[:, cut:]
    block = jnp.concatenate(rows, 0).astype(BF16)
    extra = three_rows(jnp.sum(counts, axis=0, keepdims=True), 8).astype(BF16)
    for p in range(out_ref.shape[0]):
        out_ref[p, : nz * PIECE] = block
        out_ref[p, nz * PIECE :] = extra


def fetch_activations(got_ref, h_hbm, h_ref, sem):
    fetch = pltpu.make_async_copy(h_hbm, h_ref, sem)
    fetch.start()
    fetch.wait()


def local_part(sizes, total, side_ref, got_ref, other_ref, h_ref, grad_ref, low_ref, w_ref, send_ref,
               keep_ref, probs_ref, frac_ref):
    nx, nc, nz, ny = sizes
    n_rows = nz * PIECE
    experts = got_ref.shape[2]
    low_side = side_ref[0] == 0
    counts = rows_total(got_ref[:, n_rows:]) + rows_total(other_ref[:, n_rows:])
    frac = experts * counts / (K * total)
    frac_ref[...] = frac
    for x in range(nx):
        for y in range(ny):
            for z in range(0, nz, 2):
                at = pl.ds(z * PIECE, 2 * PIECE)
                a = got_ref[x * ny + y, at].astype(F32)
                b = other_ref[x * ny + y, at].astype(F32)
                if (2 * x // nx) ^ (2 * z // nz):
                    a, b = b, a
                one = jnp.where(low_side, a, b)
                two = jnp.where(low_side, b, a)
                for i in range(2):
                    row = (((z + i) * ny + y) * nx + x) * 2 * PIECE
                    half = slice(i * PIECE, (i + 1) * PIECE)
                    w_ref[pl.ds(row, 2 * PIECE)] = jnp.concatenate([one[half], two[half]], 0).astype(BF16)
    logits = jnp.dot(h_ref[...], w_ref[...], preferred_element_type=F32)
    shifted = jnp.exp(logits - jnp.max(logits, axis=1, keepdims=True))
    scale = 1.0 / jnp.sum(shifted, axis=1, keepdims=True)
    level = jnp.sum(shifted * frac, axis=1, keepdims=True) * scale
    probs = shifted * scale
    probs_ref[...] = jnp.sum(probs, axis=0, keepdims=True)
    grad = experts * probs * (frac - level)
    grad_ref[...] = grad
    low = grad.astype(BF16)
    low_ref[...] = low
    width = 2 * ny * nx * nc * PIECE
    for z in range(0, nz, 2):
        part = lax.dot_general(
            h_ref[:, pl.ds((z // 2) * width, width)], low, (((0,), (0,)), ((), ())), preferred_element_type=F32
        )
        part = part.reshape(2, ny, nx, nc, PIECE, experts)
        for x in range(nx):
            for y in range(ny):
                c = (2 * x // nx) ^ (2 * z // nz)
                keep = [jnp.where(low_side, part[i, y, x, c], part[i, y, x, 1 - c]) for i in range(2)]
                send = [jnp.where(low_side, part[i, y, x, 1 - c], part[i, y, x, c]) for i in range(2)]
                at = pl.ds((x * ny + y) * n_rows + z * PIECE, 2 * PIECE)
                keep_ref[at] = jnp.concatenate(keep, 0)
                send_ref[at] = jnp.concatenate(send, 0).astype(BF16)
    send_ref[pl.ds(nx * ny * n_rows, 16)] = three_rows(probs_ref[...], 16).astype(BF16)


def activation_part(low_ref, w_ref, grad_ref, out_hbm, grad_hbm, out_ref, sems):
    steps = sems.shape[0] - 1
    width = out_ref.shape[1] // steps
    writes = [pltpu.make_async_copy(grad_ref, grad_hbm, sems.at[steps])]
    writes[0].start()
    for i in range(steps):
        at = pl.ds(i * width, width)
        out_ref[:, at] = lax.dot_general(
            low_ref[...], w_ref[at], (((1,), (1,)), ((), ())), preferred_element_type=F32
        ).astype(BF16)
        writes.append(pltpu.make_async_copy(out_ref.at[:, at], out_hbm.at[:, at], sems.at[i]))
        writes[-1].start()
    for write in writes:
        write.wait()


def after_core(keep_ref, came_ref, probs_ref, out_ref):
    peers, rows = out_ref.shape[0], out_ref.shape[1] - 8
    probs = probs_ref[...] + jnp.sum(came_ref[pl.ds(peers * rows, 16)].astype(F32), axis=0, keepdims=True)
    extra = three_rows(probs, 8).astype(BF16)
    for p in range(peers):
        at = pl.ds(p * rows, rows)
        out_ref[p, :rows] = (keep_ref[at] + came_ref[at].astype(F32)).astype(BF16)
        out_ref[p, rows:] = extra


def after_plane(came_ref, out_ref):
    rows = came_ref.shape[1] - 8
    extra = two_rows(rows_total(came_ref[:, rows:]))
    summed = came_ref[0, :rows].astype(F32)
    for p in range(1, came_ref.shape[0]):
        summed += came_ref[p, :rows].astype(F32)
    for z in range(out_ref.shape[0]):
        put_pairs(out_ref, z, summed[z * PIECE : (z + 1) * PIECE], extra)


def after_z(came_ref, out_ref, probs_ref):
    summed = came_ref[0].astype(F32)
    for z in range(1, came_ref.shape[0]):
        summed += came_ref[z].astype(F32)
    experts = out_ref.shape[2]
    cut = PIECE // 2 * experts
    probs_ref[...] = jnp.sum(summed[:, cut:], axis=0, keepdims=True)
    own = jnp.concatenate([summed[:, j : j + experts] for j in range(0, cut, experts)], 0)
    for p in range(out_ref.shape[0]):
        out_ref[p] = own


def last_part(total, came_ref, probs_ref, frac_ref, grad_ref, load_ref, loss_ref):
    mean = probs_ref[...] / total
    load_ref[...] = came_ref.shape[2] * mean
    loss_ref[...] = jnp.sum(frac_ref[...] * mean, axis=1, keepdims=True)
    for p in range(came_ref.shape[0]):
        grad_ref[pl.ds(p * PIECE, PIECE)] = came_ref[p]


def shards(hidden_states, router_weight, expert_ids):
    sizes = nx, nc, nz, ny = tuple(lax.axis_size(a) for a in ("x", "core", "z", "y"))
    tokens, width = hidden_states.shape
    experts = router_weight.shape[1]
    total_tokens = tokens * nx * nc * nz * ny
    core = lax.axis_index("core").astype(jnp.int32)
    place = lax.axis_index("x").astype(jnp.int32) * nc + core
    halves = 2 * lax.axis_index("x") // nx + 2 * lax.axis_index("z") // nz
    side = (core + halves.astype(jnp.int32)) % 2
    swap = [(i, nc - 1 - i) for i in range(nc)]
    plane, n_rows = nx * ny, nz * PIECE
    vm, sds = pltpu.VMEM, jax.ShapeDtypeStruct
    pairs = vm((nz, 2, (PIECE // 2 + 1) * experts), BF16)

    block = call(
        first_block,
        pairs,
        [SM, HBM, HBM],
        scratch=[vm(expert_ids.T.shape, jnp.int32), vm((2 * PIECE, experts), BF16), pltpu.SemaphoreType.DMA((2,))],
        nbytes=MIB // 4,
    )(place[None], in_hbm(expert_ids.T), in_hbm(router_weight))
    got = lax.all_to_all(block, ("core", "z"), 0, 0, axis_index_groups=crossed(nc, (nz, 1)), tiled=True)
    block = call(next_block, vm((plane, n_rows + 8, experts), BF16), [VM], nbytes=MIB)(got)
    got = lax.all_to_all(block, ("core", "x", "y"), 0, 0, axis_index_groups=crossed(nc, (nx, ny)), tiled=True)
    other = lax.ppermute(got, "core", swap)
    h_near = call(
        fetch_activations,
        vm((tokens, width), BF16),
        [VM, HBM],
        scratch=[pltpu.SemaphoreType.DMA],
        nbytes=4 * MIB,
    )(got, in_hbm(hidden_states))
    other, h_near = lax.optimization_barrier((other, h_near))

    grad_near, low, weight, sent, kept, local_probs, frac = call(
        functools.partial(local_part, sizes, total_tokens),
        (
            vm((tokens, experts), F32),
            vm((tokens, experts), BF16),
            vm((width, experts), BF16),
            vm((plane * n_rows + 16, experts), BF16),
            vm((plane * n_rows, experts), F32),
            vm((1, experts), F32),
            vm((1, experts), F32),
        ),
        [SM, VM, VM, VM],
        flops=4 * tokens * width * experts,
        nbytes=6 * MIB,
        limit=24 * MIB,
    )(side[None], got, other, h_near)

    came = lax.ppermute(sent, "core", swap)
    hidden_grad, grad_out = call(
        activation_part,
        (sds((tokens, width), BF16), sds((tokens, experts), F32)),
        [VM, VM, VM],
        outs_at=(HBM, HBM),
        scratch=[vm((tokens, width), BF16), pltpu.SemaphoreType.DMA((9,))],
        flops=2 * tokens * width * experts,
        nbytes=3 * MIB,
    )(low, weight, grad_near)
    came, hidden_grad, grad_out = lax.optimization_barrier((came, hidden_grad, grad_out))
    out = vm((plane, n_rows + 8, experts), BF16)
    block = call(after_core, out, [VM, VM, VM], nbytes=3 * MIB)(kept, came, local_probs)
    came = lax.all_to_all(block, ("core", "x", "y"), 0, 0, axis_index_groups=crossed(nc, (nx, ny)), tiled=True)
    block = call(after_plane, pairs, [VM], nbytes=MIB)(came)
    came = lax.all_to_all(block, ("core", "z"), 0, 0, axis_index_groups=crossed(nc, (nz, 1)), tiled=True)
    out = (vm((nx * nc, PIECE, experts), F32), vm((1, experts), F32))
    block, prob_total = call(after_z, out, [VM], nbytes=MIB // 8)(came)
    came = lax.all_to_all(block, ("x", "core"), 0, 0, tiled=True)
    out = (sds((nx * nc * PIECE, experts), F32), sds((1, experts), F32), sds((1, 1), F32))
    weight_grad, expert_load, balance_loss = call(
        functools.partial(last_part, total_tokens), out, [VM, VM, VM]
    )(came, prob_total, frac)
    return (balance_loss[0, 0], expert_load[0], grad_out, hidden_grad, weight_grad)


def solution(mesh):
    fine = Mesh(mesh.devices.reshape(4, 2, 16, 4), ("x", "core", "z", "y"))
    tokens = P(("x", "core", "z", "y"), None)
    rows = P(("z", "y"), None)
    return jax.shard_map(
        shards,
        mesh=fine,
        in_specs=(tokens, rows, tokens),
        out_specs=(P(), P(), tokens, tokens, rows),
        check_vma=False,
    )
```

```python
import functools

import jax
import jax.numpy as jnp
from jax import lax
from jax.experimental import pallas as pl
from jax.experimental.pallas import tpu as pltpu
from jax.sharding import Mesh, PartitionSpec as P

K = 8
F32 = jnp.float32
BF16 = jnp.bfloat16
PIECE = 8
MIB = 1 << 20


def three_rows(v, rows):
    hi = v.astype(BF16).astype(F32)
    mid = (v - hi).astype(BF16).astype(F32)
    low = v - hi - mid
    shape = (rows, v.shape[-1])
    row = lax.broadcasted_iota(jnp.int32, shape, 0)
    return jnp.where(row == 0, hi, jnp.where(row == 1, mid, jnp.where(row == 2, low, 0.0)))


def two_rows(v):
    hi = v.astype(BF16).astype(F32)
    row = lax.broadcasted_iota(jnp.int32, (2, v.shape[-1]), 0)
    return jnp.where(row == 0, hi, v - hi)


def put_pairs(out_ref, z, rows, extra):
    experts = rows.shape[1]
    for j in range(PIECE // 2):
        out_ref[z, :, j * experts : (j + 1) * experts] = rows[2 * j : 2 * j + 2].astype(BF16)
    out_ref[z, :, PIECE // 2 * experts :] = extra.astype(BF16)


def crossed(cores, nz):
    return [[(g ^ (2 * z // nz)) * nz + z for z in range(nz)] for g in range(cores)]


def rows_total(a):
    return jnp.sum(jnp.sum(a.astype(F32), axis=0), axis=0, keepdims=True)


def call(kernel, outs, ins, outs_at=None, scratch=(), flops=0, nbytes=0, limit=8 * MIB):
    return pl.pallas_call(
        kernel,
        out_shape=outs,
        in_specs=ins,
        out_specs=outs_at or jax.tree.map(lambda _: VM, outs),
        scratch_shapes=list(scratch),
        compiler_params=pltpu.CompilerParams(vmem_limit_bytes=limit),
        cost_estimate=pl.CostEstimate(flops=flops, bytes_accessed=nbytes, transcendentals=0),
    )


VM = pl.BlockSpec(memory_space=pltpu.VMEM)
SM = pl.BlockSpec(memory_space=pltpu.SMEM)
HBM = pl.BlockSpec(memory_space=pltpu.HBM)


def in_hbm(a):
    return pltpu.with_memory_space_constraint(a, pltpu.HBM)


def first_block(place_ref, ids_hbm, weight_hbm, out_ref, ids_ref, rows_ref, sems):
    pair = pl.multiple_of(place_ref[0] // 2 * (2 * PIECE), 2 * PIECE)
    fetches = [
        pltpu.make_async_copy(ids_hbm, ids_ref, sems.at[0]),
        pltpu.make_async_copy(weight_hbm.at[pl.ds(pair, 2 * PIECE)], rows_ref, sems.at[1]),
    ]
    for fetch in fetches:
        fetch.start()
    for fetch in fetches:
        fetch.wait()
    experts = rows_ref.shape[1]
    expert = lax.broadcasted_iota(jnp.int32, (experts, ids_ref.shape[1]), 0)
    hits = jnp.zeros(expert.shape, F32)
    for k in range(ids_ref.shape[0]):
        hits += jnp.where(ids_ref[k : k + 1] == expert, 1.0, 0.0)
    counts = lax.dot_general(
        jnp.ones((8, ids_ref.shape[1]), BF16),
        hits.astype(BF16),
        (((1,), (1,)), ((), ())),
        preferred_element_type=F32,
    )[:1]
    rows = rows_ref[...].astype(F32)
    mine = jnp.where(place_ref[0] % 2 == 0, rows[:PIECE], rows[PIECE:])
    extra = two_rows(counts)
    for z in range(out_ref.shape[0]):
        put_pairs(out_ref, z, mine, extra)


def next_block(came_ref, out_ref):
    nz, experts = came_ref.shape[0], out_ref.shape[2]
    cut = PIECE // 2 * experts
    rows, counts = [], jnp.zeros((2, experts), F32)
    for z in range(nz):
        came = came_ref[z].astype(F32)
        rows += [came[:, j : j + experts] for j in range(0, cut, experts)]
        counts += came[:, cut:]
    block = jnp.concatenate(rows, 0).astype(BF16)
    extra = three_rows(jnp.sum(counts, axis=0, keepdims=True), 8).astype(BF16)
    for p in range(out_ref.shape[0]):
        out_ref[p, : nz * PIECE] = block
        out_ref[p, nz * PIECE :] = extra


def fetch_activations(got_ref, h_hbm, h_ref, sem):
    fetch = pltpu.make_async_copy(h_hbm, h_ref, sem)
    fetch.start()
    fetch.wait()


def local_part(sizes, total, side_ref, got_ref, other_ref, h_ref, grad_hbm, low_ref, w_ref, send_ref,
               keep_ref, probs_ref, frac_ref, grad_ref, sem):
    nx, nc, nz, ny = sizes
    n_rows = nz * PIECE
    experts = got_ref.shape[2]
    low_side = side_ref[0] == 0
    counts = rows_total(got_ref[:, n_rows:]) + rows_total(other_ref[:, n_rows:])
    frac = experts * counts / (K * total)
    frac_ref[...] = frac
    for x in range(nx):
        for y in range(ny):
            for z in range(0, nz, 2):
                at = pl.ds(z * PIECE, 2 * PIECE)
                a = got_ref[x * ny + y, at].astype(F32)
                b = other_ref[x * ny + y, at].astype(F32)
                if 2 * z // nz:
                    a, b = b, a
                one = jnp.where(low_side, a, b)
                two = jnp.where(low_side, b, a)
                for i in range(2):
                    row = (((z + i) * ny + y) * nx + x) * 2 * PIECE
                    half = slice(i * PIECE, (i + 1) * PIECE)
                    w_ref[pl.ds(row, 2 * PIECE)] = jnp.concatenate([one[half], two[half]], 0).astype(BF16)
    logits = jnp.dot(h_ref[...], w_ref[...], preferred_element_type=F32)
    shifted = jnp.exp(logits - jnp.max(logits, axis=1, keepdims=True))
    probs = shifted / jnp.sum(shifted, axis=1, keepdims=True)
    probs_ref[...] = jnp.sum(probs, axis=0, keepdims=True)
    level = jnp.sum(probs * frac, axis=1, keepdims=True)
    grad = experts * probs * (frac - level)
    grad_ref[...] = grad
    write = pltpu.make_async_copy(grad_ref, grad_hbm, sem)
    write.start()
    low = grad.astype(BF16)
    low_ref[...] = low
    width = 2 * ny * nx * nc * PIECE
    for z in range(0, nz, 2):
        part = lax.dot_general(
            h_ref[:, pl.ds((z // 2) * width, width)], low, (((0,), (0,)), ((), ())), preferred_element_type=F32
        )
        part = part.reshape(2, ny, nx, nc, PIECE, experts)
        for x in range(nx):
            for y in range(ny):
                c = 2 * z // nz
                keep = [jnp.where(low_side, part[i, y, x, c], part[i, y, x, 1 - c]) for i in range(2)]
                send = [jnp.where(low_side, part[i, y, x, 1 - c], part[i, y, x, c]) for i in range(2)]
                at = pl.ds((x * ny + y) * n_rows + z * PIECE, 2 * PIECE)
                keep_ref[at] = jnp.concatenate(keep, 0)
                send_ref[at] = jnp.concatenate(send, 0).astype(BF16)
    send_ref[pl.ds(nx * ny * n_rows, 16)] = three_rows(probs_ref[...], 16).astype(BF16)
    write.wait()


def activation_part(low_ref, w_ref, out_hbm, out_ref, sems):
    width = out_ref.shape[1] // sems.shape[0]
    writes = []
    for i in range(sems.shape[0]):
        at = pl.ds(i * width, width)
        out_ref[:, at] = lax.dot_general(
            low_ref[...], w_ref[at], (((1,), (1,)), ((), ())), preferred_element_type=F32
        ).astype(BF16)
        writes.append(pltpu.make_async_copy(out_ref.at[:, at], out_hbm.at[:, at], sems.at[i]))
        writes[-1].start()
    for write in writes:
        write.wait()


def after_core(keep_ref, came_ref, probs_ref, out_ref):
    peers, rows = out_ref.shape[0], out_ref.shape[1] - 8
    probs = probs_ref[...] + jnp.sum(came_ref[pl.ds(peers * rows, 16)].astype(F32), axis=0, keepdims=True)
    extra = three_rows(probs, 8).astype(BF16)
    for p in range(peers):
        at = pl.ds(p * rows, rows)
        out_ref[p, :rows] = (keep_ref[at] + came_ref[at].astype(F32)).astype(BF16)
        out_ref[p, rows:] = extra


def after_plane(came_ref, out_ref):
    rows = came_ref.shape[1] - 8
    extra = two_rows(rows_total(came_ref[:, rows:]))
    summed = came_ref[0, :rows].astype(F32)
    for p in range(1, came_ref.shape[0]):
        summed += came_ref[p, :rows].astype(F32)
    for z in range(out_ref.shape[0]):
        put_pairs(out_ref, z, summed[z * PIECE : (z + 1) * PIECE], extra)


def after_z(came_ref, out_ref, probs_ref):
    summed = came_ref[0].astype(F32)
    for z in range(1, came_ref.shape[0]):
        summed += came_ref[z].astype(F32)
    experts = out_ref.shape[2]
    cut = PIECE // 2 * experts
    probs_ref[...] = jnp.sum(summed[:, cut:], axis=0, keepdims=True)
    own = jnp.concatenate([summed[:, j : j + experts] for j in range(0, cut, experts)], 0)
    for p in range(out_ref.shape[0]):
        out_ref[p] = own


def last_part(total, came_ref, probs_ref, frac_ref, grad_ref, load_ref, loss_ref):
    mean = probs_ref[...] / total
    load_ref[...] = came_ref.shape[2] * mean
    loss_ref[...] = jnp.sum(frac_ref[...] * mean, axis=1, keepdims=True)
    for p in range(came_ref.shape[0]):
        grad_ref[pl.ds(p * PIECE, PIECE)] = came_ref[p]


def shards(hidden_states, router_weight, expert_ids):
    sizes = nx, nc, nz, ny = tuple(lax.axis_size(a) for a in ("x", "core", "z", "y"))
    tokens, width = hidden_states.shape
    experts = router_weight.shape[1]
    total_tokens = tokens * nx * nc * nz * ny
    core = lax.axis_index("core").astype(jnp.int32)
    place = lax.axis_index("x").astype(jnp.int32) * nc + core
    side = (core + (2 * lax.axis_index("z") // nz).astype(jnp.int32)) % 2
    swap = [(i, nc - 1 - i) for i in range(nc)]
    plane, n_rows = nx * ny, nz * PIECE
    vm, sds = pltpu.VMEM, jax.ShapeDtypeStruct
    pairs = vm((nz, 2, (PIECE // 2 + 1) * experts), BF16)

    block = call(
        first_block,
        pairs,
        [SM, HBM, HBM],
        scratch=[vm(expert_ids.T.shape, jnp.int32), vm((2 * PIECE, experts), BF16), pltpu.SemaphoreType.DMA((2,))],
        nbytes=MIB // 4,
    )(place[None], in_hbm(expert_ids.T), in_hbm(router_weight))
    got = lax.all_to_all(block, ("core", "z"), 0, 0, axis_index_groups=crossed(nc, nz), tiled=True)
    block = call(next_block, vm((plane, n_rows + 8, experts), BF16), [VM], nbytes=MIB)(got)
    got = lax.all_to_all(block, ("x", "y"), 0, 0, tiled=True)
    other = lax.ppermute(got, "core", swap)
    h_near = call(
        fetch_activations,
        vm((tokens, width), BF16),
        [VM, HBM],
        scratch=[pltpu.SemaphoreType.DMA],
        nbytes=4 * MIB,
    )(got, in_hbm(hidden_states))
    other, h_near = lax.optimization_barrier((other, h_near))

    grad_out, low, weight, sent, kept, local_probs, frac = call(
        functools.partial(local_part, sizes, total_tokens),
        (
            sds((tokens, experts), F32),
            vm((tokens, experts), BF16),
            vm((width, experts), BF16),
            vm((plane * n_rows + 16, experts), BF16),
            vm((plane * n_rows, experts), F32),
            vm((1, experts), F32),
            vm((1, experts), F32),
        ),
        [SM, VM, VM, VM],
        outs_at=(HBM,) + (VM,) * 6,
        scratch=[vm((tokens, experts), F32), pltpu.SemaphoreType.DMA],
        flops=4 * tokens * width * experts,
        nbytes=6 * MIB,
        limit=24 * MIB,
    )(side[None], got, other, h_near)

    came = lax.ppermute(sent, "core", swap)
    hidden_grad = call(
        activation_part,
        sds((tokens, width), BF16),
        [VM, VM],
        outs_at=HBM,
        scratch=[vm((tokens, width), BF16), pltpu.SemaphoreType.DMA((8,))],
        flops=2 * tokens * width * experts,
        nbytes=3 * MIB,
    )(low, weight)
    came, hidden_grad = lax.optimization_barrier((came, hidden_grad))
    out = vm((plane, n_rows + 8, experts), BF16)
    block = call(after_core, out, [VM, VM, VM], nbytes=3 * MIB)(kept, came, local_probs)
    came = lax.all_to_all(block, ("x", "y"), 0, 0, tiled=True)
    block = call(after_plane, pairs, [VM], nbytes=MIB)(came)
    came = lax.all_to_all(block, ("core", "z"), 0, 0, axis_index_groups=crossed(nc, nz), tiled=True)
    out = (vm((nx * nc, PIECE, experts), F32), vm((1, experts), F32))
    block, prob_total = call(after_z, out, [VM], nbytes=MIB // 8)(came)
    came = lax.all_to_all(block, ("x", "core"), 0, 0, tiled=True)
    out = (sds((nx * nc * PIECE, experts), F32), sds((1, experts), F32), sds((1, 1), F32))
    weight_grad, expert_load, balance_loss = call(
        functools.partial(last_part, total_tokens), out, [VM, VM, VM]
    )(came, prob_total, frac)
    return (balance_loss[0, 0], expert_load[0], grad_out, hidden_grad, weight_grad)


def solution(mesh):
    fine = Mesh(mesh.devices.reshape(4, 2, 16, 4), ("x", "core", "z", "y"))
    tokens = P(("x", "core", "z", "y"), None)
    rows = P(("z", "y"), None)
    return jax.shard_map(
        shards,
        mesh=fine,
        in_specs=(tokens, rows, tokens),
        out_specs=(P(), P(), tokens, tokens, rows),
        check_vma=False,
    )
```
